512 devices in a mesh: seq: 64 (over x, z_hi, y, core), head: 8 (over z_lo).
Axes of the slice: x: 4, y: 4, z: 16 (z_hi: 2, z_lo: 8; z = z_hi * 8 + z_lo), core: 2. Of those that a mesh axis runs over, the one named last changes fastest.
Arguments:
- queries: bfloat16 [32768, 3072], P('seq', 'head'), may hold values from -120 to 120
- encodings: bfloat16 [64, 256, 4096], P('seq', None, 'head'), may hold values from -6 to 6
- key_weight: bfloat16 [4096, 3072], P('seq', 'head'), may hold values from -0.09375 to 0.09375
- value_weight: bfloat16 [4096, 3072], P('seq', 'head'), may hold values from -0.09375 to 0.09375
- text_length: int32 [64], P('seq'), may hold values from 1 to 256
- image_offset: int32 [64], P('seq'), may hold values from 0 to 511, as said below
- cotangent: bfloat16 [32768, 3072], P('seq', 'head'), may hold values from -6 to 6
Outputs:
- attended: bfloat16 [32768, 3072], P('seq', 'head')
- query_grad: bfloat16 [32768, 3072], P('seq', 'head')
- encoding_grad: bfloat16 [64, 256, 4096], P('seq', None, 'head')
The draws below stay inside these ranges and needn't reach their ends.
Inputs may be any that keep to these rules, and one draw needn't show every extreme that they name: The image tokens of prompt p begin at p * 512 + image_offset[p] and run up to where those of prompt p + 1 begin, the last prompt's to the end; image_offset[0] is 0.
All inputs are finite; a program needn't handle non-finite values.
Results may differ from the reference program's by a relative error of at most 0.018.
The reference program's roundings to bfloat16 on the way (of `keys`, `values`, `probs_b`, `dscores`, `key_grad` and `value_grad`) count: a program that leaves them out, or rounds other values in their place, can miss the bound.
Values may be sent and summed in bfloat16 or wider, within the bound.
A program may use at most 64 MiB of HBM per device.

```python
import math
import jax
import jax.numpy as jnp
from jax import lax

HEADS = 24
HD = 128
D = 3072
DT = 4096
TOK_DEV = 512
LMAX = 256
PROMPTS = 64
TOKENS = 32768
N_HEAD = 8


def draw_queries(key, part):
    key = jax.random.fold_in(key, 3)
    first = jax.random.fold_in(key, 0)
    values = jnp.clip(jax.random.normal(first, (TOKENS, D), jnp.float32), -6.0, 6.0)
    return values.astype(jnp.bfloat16)


def draw_text_length(key, part):
    key = jax.random.fold_in(key, 5)
    first, second = jax.random.split(key)
    lengths = jax.random.randint(first, (PROMPTS,), 1, LMAX + 1)
    where_full = jax.random.randint(second, (), 0, PROMPTS)
    return lengths.at[where_full].set(LMAX).astype(jnp.int32)


def draw_image_offset(key, part):
    key = jax.random.fold_in(key, 7)
    first, second = jax.random.split(key)
    offsets = jax.random.randint(first, (PROMPTS,), 0, TOK_DEV)
    where_last = jax.random.randint(second, (), 1, PROMPTS)
    offsets = offsets.at[where_last].set(TOK_DEV - 1)
    return offsets.at[0].set(0).astype(jnp.int32)


def steps_of(key, extent, shards, smallest, high):
    def one(position, shards_of):
        steps = jax.random.uniform(jax.random.fold_in(jax.random.fold_in(key, 6), position), (shards_of,), jnp.float32, smallest / len(shards), high / len(shards))
        return jnp.repeat(jnp.exp(steps), extent[position] // shards_of).reshape((-1,) + (1,) * (len(extent) - position - 1))

    gain = one(*shards[0])
    for cut in shards[1:]:
        gain = gain * one(*cut)
    return gain


def normal_values(stream_key, extent, width, bound, pieces=(), kind=jnp.bfloat16):
    entries = jax.random.normal(stream_key, extent, jnp.float32) * width
    if len(pieces) > 0:
        entries = steps_of(stream_key, extent, pieces, -0.22, 0.18) * entries
    return jnp.clip(entries, min=-bound, max=bound).astype(kind)


def setup_inputs(seed: int = 0) -> dict:
    seeds = jax.random.split(jax.random.key(seed), 8)
    return {
        "queries": draw_queries(jax.random.fold_in(seeds[7], 71), 0),
        "encodings": normal_values(seeds[1], (PROMPTS, LMAX, DT), 1.0, 6.0, ((0, 64), (2, 8))),
        "key_weight": normal_values(seeds[2], (DT, D), DT ** -0.5, 0.09375, ((0, 64), (1, 8))),
        "value_weight": normal_values(seeds[3], (DT, D), DT ** -0.5, 0.09375, ((0, 64), (1, 8))),
        "text_length": draw_text_length(jax.random.fold_in(seeds[7], 71), 0),
        "image_offset": draw_image_offset(jax.random.fold_in(seeds[7], 71), 0),
        "cotangent": normal_values(seeds[6], (TOKENS, D), 1.0, 6.0, ((0, 64), (1, 8))),
    }


def attend(q, g, keys, values, allowed):
    scale = 1.0 / math.sqrt(HD)
    qf = q.astype(jnp.float32)
    gf = g.astype(jnp.float32)
    kf = keys.astype(jnp.float32)
    vf = values.astype(jnp.float32)
    scores = jnp.einsum('thd,khd->htk', qf, kf) * scale
    masked = jnp.where(allowed[None], scores, jnp.float32(-1e+30))
    top = lax.optimization_barrier(jnp.max(masked, axis=-1, keepdims=True))
    expo = jnp.exp(masked - top)
    probs = expo / lax.optimization_barrier(jnp.sum(expo, axis=-1, keepdims=True))
    probs_b = probs.astype(jnp.bfloat16).astype(jnp.float32)
    out = jnp.einsum('htk,khd->thd', probs_b, vf).astype(jnp.bfloat16)
    dprobs = jnp.einsum('thd,khd->htk', gf, vf)
    delta = lax.optimization_barrier(jnp.sum(probs * dprobs, axis=-1, keepdims=True))
    dscores = (probs * (dprobs - delta) * scale).astype(jnp.bfloat16).astype(jnp.float32)
    dq = jnp.einsum('htk,khd->thd', dscores, kf).astype(jnp.bfloat16)
    dk = jnp.einsum('htk,thd->khd', dscores, qf)
    dv = jnp.einsum('htk,thd->khd', probs_b, gf)
    return (out, dq, dk, dv)

def reference(queries, encodings, key_weight, value_weight, text_length, image_offset, cotangent):
    flat = encodings.reshape(PROMPTS * LMAX, DT)
    keys = jnp.dot(flat, key_weight, preferred_element_type=jnp.float32).astype(jnp.bfloat16).reshape(PROMPTS, LMAX, HEADS, HD)
    values = jnp.dot(flat, value_weight, preferred_element_type=jnp.float32).astype(jnp.bfloat16).reshape(PROMPTS, LMAX, HEADS, HD)
    valid = jnp.arange(LMAX, dtype=jnp.int32)[None, :] < text_length[:, None]
    keys_prev = jnp.concatenate([jnp.zeros_like(keys[:1]), keys[:-1]], 0)
    values_prev = jnp.concatenate([jnp.zeros_like(values[:1]), values[:-1]], 0)
    valid_prev = jnp.concatenate([jnp.zeros_like(valid[:1]), valid[:-1]], 0)
    qs = queries.reshape(PROMPTS, TOK_DEV, HEADS, HD)
    gs = cotangent.reshape(PROMPTS, TOK_DEV, HEADS, HD)

    def one_block(items):
        q, g, kp, ko, vp, vo, okp, oko, offset = items
        rows = jnp.arange(TOK_DEV, dtype=jnp.int32)
        own_row = (rows >= offset)[:, None]
        allowed = jnp.concatenate([jnp.logical_and(jnp.logical_not(own_row), okp[None, :]), jnp.logical_and(own_row, oko[None, :])], 1)
        return attend(q, g, jnp.concatenate([kp, ko], 0), jnp.concatenate([vp, vo], 0), allowed)
    out, dq, dk, dv = lax.map(one_block, (qs, gs, keys_prev, keys, values_prev, values, valid_prev, valid, image_offset))
    dk_own = dk[:, LMAX:]
    dv_own = dv[:, LMAX:]
    dk_back = jnp.concatenate([dk[1:, :LMAX], jnp.zeros_like(dk[:1, :LMAX])], 0)
    dv_back = jnp.concatenate([dv[1:, :LMAX], jnp.zeros_like(dv[:1, :LMAX])], 0)
    key_grad = (dk_own + dk_back).astype(jnp.bfloat16).reshape(PROMPTS * LMAX, D)
    value_grad = (dv_own + dv_back).astype(jnp.bfloat16).reshape(PROMPTS * LMAX, D)
    group = D // N_HEAD
    total = jnp.zeros((PROMPTS * LMAX, DT), jnp.float32)
    for index in range(N_HEAD):
        lo = index * group
        part = lax.dot_general(key_grad[:, lo:lo + group], key_weight[:, lo:lo + group], (((1,), (1,)), ((), ())), preferred_element_type=jnp.float32)
        part = part + lax.dot_general(value_grad[:, lo:lo + group], value_weight[:, lo:lo + group], (((1,), (1,)), ((), ())), preferred_element_type=jnp.float32)
        total = total + part.astype(jnp.bfloat16).astype(jnp.float32)
    encoding_grad = total.astype(jnp.bfloat16).reshape(PROMPTS, LMAX, DT)
    return (out.reshape(TOKENS, D), dq.reshape(TOKENS, D), encoding_grad)
```

```python
import functools
import math

import jax
import jax.numpy as jnp
from jax import lax
from jax.experimental import pallas as pl
from jax.experimental.pallas import tpu as pltpu
from jax.sharding import PartitionSpec as P

HD = 128
GRID = (4, 2, 4, 2)
CHUNKS = 2
BF = jnp.bfloat16
F32 = jnp.float32
MESH = pl.DeviceIdType.MESH


def dot(a, b, da, db):
    return lax.dot_general(a, b, (((da,), (db,)), ((), ())), preferred_element_type=F32)


def kernel(
    dims, len_ref, off_ref, q_ref, g_ref, enc_ref, wk_ref, wv_ref,
    out_ref, dq_ref, de_ref,
    w, wmid, enc, kv, valid, ra, rm, rc, ba, bm, bc, dk32, dprev, dback, dkv, rr, rl, proj,
    ws1, wr1, ws2, wr2, wsx, wrx, wsb, wrb,
    esr, err, esl, erl, vs, vr,
    ks, kr, ps, pr, cs, cr, fs, fr,
    bks, bkr, bps, bpr, bcs, bcr, bfs, bfr,
    rsr, rrr, rsl, rrl,
):
    nx, nh, ny, nc, nz = dims
    width = wk_ref.shape[1]
    heads = width // HD
    lmax = enc_ref.shape[1]
    tokens = q_ref.shape[0]
    piece = lmax // ny
    rows = lmax // CHUNKS
    s = lax.axis_index("seq")
    h = lax.axis_index("head")
    c = s % nc
    y = (s // nc) % ny
    zh = (s // (nc * ny)) % nh
    x = s // (nc * ny * nh)
    last = nx * nh * ny * nc - 1

    def at(x_, zh_, y_, c_):
        return ((x_ * nh + zh_) * ny + y_) * nc + c_

    def along(steps):
        z = (zh * nz + h + steps + nh * nz) % (nh * nz)
        return (at(x, z // nz, y, c), z % nz), z // nz

    sib = (at(x, zh, y, 1 - c), h)
    up, zh_up = along(nz // 2)
    down, zh_down = along(-(nz // 2))
    xs = [(at((x + d) % nx, zh, y, c), h) for d in range(1, nx)]
    ys = [(at(x, zh, (y + d) % ny, c), h) for d in range(1, ny)]
    right = (s, h + 1)
    left = (s, h - 1)
    KC, VC = slice(0, width), slice(width, 2 * width)

    has_next = s < last
    has_prev = s > 0
    far_next = jnp.logical_and(c == nc - 1, y == ny - 1)
    far_prev = jnp.logical_and(c == 0, y == 0)
    relay = c == nc - 1
    serves = jnp.logical_and(relay, jnp.logical_or(zh == 1, x < nx - 1))
    served_x = jnp.where(zh == 1, x, x + 1)
    goes = jnp.logical_and(relay, jnp.logical_not(jnp.logical_and(zh == 1, x == nx - 1)))
    source_x = jnp.where(zh == 1, x, x - 1)

    def when(*conds):
        return pl.when(functools.reduce(jnp.logical_and, conds))

    def copy(src, dst, ss, rs, dev):
        return pltpu.make_async_remote_copy(
            src_ref=src, dst_ref=dst, send_sem=ss, recv_sem=rs, device_id=dev, device_id_type=MESH
        )

    barrier = pltpu.get_barrier_semaphore()

    def hello(dev):
        pl.semaphore_signal(barrier, inc=1, device_id=dev, device_id_type=MESH)

    for dev in [sib, up, down] + xs + ys:
        hello(dev)

    @when(h < nz - 1)
    def _():
        hello(right)

    @when(h > 0)
    def _():
        hello(left)

    @when(has_next)
    def _():
        hello((s + 1, h))

    @when(has_prev)
    def _():
        hello((s - 1, h))

    @when(serves)
    def _():
        hello((at(served_x, zh, 0, 0), h))

    @when(far_prev, has_prev)
    def _():
        for i in range(ny):
            hello((at(source_x, zh, i, nc - 1), h))

    w[x, zh, y, c, :, KC] = wk_ref[...]
    w[x, zh, y, c, :, VC] = wv_ref[...]
    enc[h] = enc_ref[0]
    columns = lax.broadcasted_iota(jnp.int32, (8, lmax), 1)
    valid[1] = (columns < len_ref[0]).astype(F32)

    @when(s == 0)
    def _():
        valid[0] = jnp.ones((8, lmax), F32)
        kv[0] = jnp.zeros((lmax, 2 * width), BF)

    @when(s == last)
    def _():
        dback[...] = jnp.zeros_like(dback)

    @when(h == 0)
    def _():
        rr[...] = jnp.zeros_like(rr)

    @when(h == nz - 1)
    def _():
        rl[...] = jnp.zeros_like(rl)

    count = 3 + (nx - 1) + (ny - 1)
    count = count + (h < nz - 1).astype(jnp.int32) + (h > 0).astype(jnp.int32)
    count = count + has_next.astype(jnp.int32) + has_prev.astype(jnp.int32)
    count = count + serves.astype(jnp.int32)
    count = count + ny * jnp.logical_and(far_prev, has_prev).astype(jnp.int32)
    pl.semaphore_wait(barrier, count)

    def cross_up(i, leg):
        if i == 0:
            if leg == 0:
                return copy(w.at[x, zh, y, c, :, KC], wmid.at[:, KC], wsx.at[0], wrx.at[0], up)
            return copy(wmid.at[:, KC], w.at[x, zh_down, y, c, :, KC], wsx.at[1], wrx.at[1], up)
        if leg == 0:
            return copy(w.at[x, zh, y, c, :, VC], wmid.at[:, VC], wsx.at[2], wrx.at[2], down)
        return copy(wmid.at[:, VC], w.at[x, zh_up, y, c, :, VC], wsx.at[3], wrx.at[3], down)

    def first(which, z_, d):
        if which == 0:
            ref = w.at[x, z_, y, c, :, KC]
            return copy(ref, ref, ws1.at[0, d - 1, z_], wr1.at[0, d - 1, z_], xs[d - 1])
        ref = w.at[x, z_, y, c, :, VC]
        return copy(ref, ref, ws1.at[1, d - 1, z_], wr1.at[1, d - 1, z_], ys[d - 1])

    def second(which, z_, d):
        if which == 0:
            ref = w.at[:, z_, y, c, :, KC]
            return copy(ref, ref, ws2.at[0, d - 1, z_], wr2.at[0, d - 1, z_], ys[d - 1])
        ref = w.at[x, z_, :, c, :, VC]
        return copy(ref, ref, ws2.at[1, d - 1, z_], wr2.at[1, d - 1, z_], xs[d - 1])

    def share(z_):
        ref = w.at[:, z_, :, c]
        return copy(ref, ref, wsb.at[z_], wrb.at[z_], sib)

    def each(make, z_, act):
        for d in range(1, max(nx, ny)):
            for which in (0, 1):
                if d < (nx, ny)[which if make is first else 1 - which]:
                    act(make(which, z_, d))

    def start(cp):
        cp.start()

    def arrived(cp):
        cp.wait_recv()

    def sent(cp):
        cp.wait_send()

    def send_enc_right(j, r):
        ref = enc.at[j, pl.ds(r * rows, rows)]
        return copy(ref, ref, esr.at[j, r], err.at[j, r], right)

    def send_enc_left(j, r):
        ref = enc.at[j, pl.ds(r * rows, rows)]
        return copy(ref, ref, esl.at[j, r], erl.at[j, r], left)

    def send_valid():
        return copy(valid.at[1], valid.at[0], vs.at[0], vr.at[0], (s + 1, h))

    other = 1 - zh

    def weights_a():
        each(first, zh, start)
        for i in (0, 1):
            cross_up(i, 0).start()

    def weights_b():
        for i in (0, 1):
            cross_up(i, 0).wait_recv()
            cross_up(i, 1).start()
        each(first, zh, arrived)
        each(second, zh, start)

    def weights_c():
        for i in (0, 1):
            cross_up(i, 1).wait_recv()
        each(first, other, start)

    def weights_d():
        each(second, zh, arrived)
        share(zh).start()
        each(first, other, arrived)
        each(second, other, start)

    def weights_e():
        each(second, other, arrived)
        share(other).start()

    weights_a()

    @when(has_next)
    def _():
        send_valid().start()

    todo = {1: weights_b, 2: weights_c, 3: weights_d, 5: weights_e}
    steps = nz - 1
    for st in range(nz):
        for r in range(CHUNKS):
            if st > 0:

                @when(h - st >= 0)
                def _():
                    send_enc_right(h - st, r).wait_recv()

            if st < steps:

                @when(h - st >= 0, h < nz - 1)
                def _():
                    send_enc_right(h - st, r).start()

            if st > 0:

                @when(h + st < nz)
                def _():
                    send_enc_left(h + st, r).wait_recv()

            if st < steps:

                @when(h + st < nz, h > 0)
                def _():
                    send_enc_left(h + st, r).start()

        if st in todo:
            todo[st]()
    for st in sorted(todo):
        if st >= nz:
            todo[st]()
    share(zh).wait_recv()
    share(other).wait_recv()

    proj[...] = jnp.zeros_like(proj)

    def project(f, carry):
        block = w[f // nh, f % nh].reshape(-1, 2 * width)
        proj[...] += dot(enc[f], block, 1, 0)
        return carry

    lax.fori_loop(0, nz, project, 0)
    kv[1] = proj[...].astype(BF)

    def kv_direct():
        return copy(kv.at[1], kv.at[0], ks.at[0], kr.at[0], (s + 1, h))

    def kv_part(i):
        return copy(kv.at[1, pl.ds(i * piece, piece)], ra, ps.at[i], pr.at[0], (at(x, zh, i, nc - 1), h))

    def crossing(src, mid, dst, ss, rs, i, leg):
        cols, dev = (KC, up) if i == 0 else (VC, down)
        a, b = (src, mid) if leg == 0 else (mid, dst)
        return copy(a.at[:, cols], b.at[:, cols], ss.at[i, leg], rs.at[i, leg], dev)

    def cross_all(src, mid, dst, ss, rs):
        for i in (0, 1):
            crossing(src, mid, dst, ss, rs, i, 0).start()
        for i in (0, 1):
            crossing(src, mid, dst, ss, rs, i, 0).wait_recv()
            crossing(src, mid, dst, ss, rs, i, 1).start()
        for i in (0, 1):
            crossing(src, mid, dst, ss, rs, i, 1).wait_recv()

    def kv_final():
        return copy(rc, kv.at[0, pl.ds(pl.multiple_of(y * piece, piece), piece)], fs.at[0], fr.at[y], (at(served_x, zh, 0, 0), h))

    @when(has_next, jnp.logical_not(far_next))
    def _():
        kv_direct().start()

    @when(far_next)
    def _():
        for i in range(ny - 1):
            kv_part(i).start()
        ra[...] = kv[1, (ny - 1) * piece :]

    @when(relay)
    def _():
        @when(y < ny - 1)
        def _():
            kv_part(0).wait_recv()

        cross_all(ra, rm, rc, cs, cr)

        @when(serves)
        def _():
            kv_final().start()

    @when(has_prev)
    def _():
        send_valid().wait_recv()

        @when(jnp.logical_not(far_prev))
        def _():
            kv_direct().wait_recv()

        @when(far_prev)
        def _():
            for i in range(ny):
                copy(rc, kv.at[0, pl.ds(i * piece, piece)], fs.at[0], fr.at[i], sib).wait_recv()

    scale = 1.0 / math.sqrt(HD)
    own = lax.broadcasted_iota(jnp.int32, (tokens, lmax), 0) >= off_ref[0]
    ok = jnp.where(own, valid[1, 0:1, :], valid[0, 0:1, :]) > 0.5
    for a in range(heads):
        kc = slice(a * HD, (a + 1) * HD)
        vc = slice(width + a * HD, width + (a + 1) * HD)
        q = q_ref[:, kc]
        g = g_ref[:, kc]
        k = kv[:, :, kc].reshape(2 * lmax, HD)
        v = kv[:, :, vc].reshape(2 * lmax, HD)
        both = dot(q, k, 1, 1)
        scores = jnp.where(own, both[:, lmax:], both[:, :lmax]) * scale
        scores = jnp.where(ok, scores, -1e30)
        expo = jnp.exp(scores - jnp.max(scores, axis=-1, keepdims=True))
        probs = expo / jnp.sum(expo, axis=-1, keepdims=True)
        both = dot(g, v, 1, 1)
        dprobs = jnp.where(own, both[:, lmax:], both[:, :lmax])
        delta = jnp.sum(probs * dprobs, axis=-1, keepdims=True)
        ds = probs * (dprobs - delta) * scale
        pc = jnp.concatenate([jnp.where(own, 0.0, probs), jnp.where(own, probs, 0.0)], axis=1).astype(BF)
        dc = jnp.concatenate([jnp.where(own, 0.0, ds), jnp.where(own, ds, 0.0)], axis=1).astype(BF)
        out_ref[:, kc] = dot(pc, v, 1, 0).astype(BF)
        dq_ref[:, kc] = dot(dc, k, 1, 0).astype(BF)
        dk = dot(dc, q, 0, 0)
        dv = dot(pc, g, 0, 0)
        dprev[:, kc] = dk[:lmax].astype(BF)
        dprev[:, vc] = dv[:lmax].astype(BF)
        dk32[:, kc] = dk[lmax:]
        dk32[:, vc] = dv[lmax:]

    def back_direct():
        return copy(dprev, dback, bks.at[0], bkr.at[0], (s - 1, h))

    def back_part(i):
        return copy(dprev.at[pl.ds(i * piece, piece)], ba, bps.at[i], bpr.at[0], (at(source_x, zh, i, nc - 1), h))

    def back_final():
        return copy(bc, dback.at[pl.ds(pl.multiple_of(y * piece, piece), piece)], bfs.at[0], bfr.at[y], (at(x, zh, ny - 1, nc - 1), h))

    @when(has_prev, jnp.logical_not(far_prev))
    def _():
        back_direct().start()

    @when(has_prev, far_prev)
    def _():
        for i in range(ny):
            back_part(i).start()

    @when(relay)
    def _():
        @when(serves)
        def _():
            back_part(0).wait_recv()

        @when(jnp.logical_not(serves))
        def _():
            ba[...] = jnp.zeros_like(ba)

        cross_all(ba, bm, bc, bcs, bcr)

        @when(goes, y < ny - 1)
        def _():
            back_final().start()

        @when(goes, y == ny - 1)
        def _():
            dback[(ny - 1) * piece :, :] = bc[...]

    @when(has_next)
    def _():
        @when(jnp.logical_not(far_next))
        def _():
            back_direct().wait_recv()

        @when(far_next)
        def _():
            for i in range(ny - 1):
                copy(bc, dback.at[pl.ds(i * piece, piece)], bfs.at[0], bfr.at[i], sib).wait_recv()

    dkv[...] = (dk32[...] + dback[...].astype(F32)).astype(BF)

    def sum_right(j, r):
        ref = rr.at[j, pl.ds(r * rows, rows)]
        return copy(ref, ref, rsr.at[j, r], rrr.at[j, r], right)

    def sum_left(j, r):
        ref = rl.at[j, pl.ds(r * rows, rows)]
        return copy(ref, ref, rsl.at[j, r], rrl.at[j, r], left)

    def partial(j, r):
        block = w[j // nh, j % nh].reshape(-1, 2 * width)
        return dot(dkv[pl.ds(r * rows, rows), :], block, 1, 1)

    def reduce_step(t, carry):
        for r in range(CHUNKS):
            here = pl.ds(r * rows, rows)

            @when(t >= h, h < nz - 1)
            def _():
                j = nz - 1 + h - t
                part = partial(j, r)

                @when(h > 0)
                def _():
                    sum_right(j, r).wait_recv()

                rr[j, here, :] = (part + rr[j, here, :].astype(F32)).astype(BF)
                sum_right(j, r).start()

            @when(t >= nz - 1 - h, h > 0)
            def _():
                j = t - (nz - 1 - h)
                part = partial(j, r)

                @when(h < nz - 1)
                def _():
                    sum_left(j, r).wait_recv()

                rl[j, here, :] = (part + rl[j, here, :].astype(F32)).astype(BF)
                sum_left(j, r).start()

        return carry

    lax.fori_loop(0, nz - 1, reduce_step, 0)

    for r in range(CHUNKS):
        here = pl.ds(r * rows, rows)
        part = partial(h, r)

        @when(h > 0)
        def _():
            sum_right(h, r).wait_recv()

        @when(h < nz - 1)
        def _():
            sum_left(h, r).wait_recv()

        total = part + rr[h, here, :].astype(F32) + rl[h, here, :].astype(F32)
        de_ref[0, here, :] = total.astype(BF)

    each(first, 0, sent)
    each(first, 1, sent)
    each(second, 0, sent)
    each(second, 1, sent)
    share(0).wait_send()
    share(1).wait_send()
    for i in (0, 1):
        for leg in (0, 1):
            cross_up(i, leg).wait_send()

    @when(has_next)
    def _():
        send_valid().wait_send()

    @when(has_next, jnp.logical_not(far_next))
    def _():
        kv_direct().wait_send()

    @when(far_next)
    def _():
        for i in range(ny - 1):
            kv_part(i).wait_send()

    @when(has_prev, jnp.logical_not(far_prev))
    def _():
        back_direct().wait_send()

    @when(has_prev, far_prev)
    def _():
        for i in range(ny):
            back_part(i).wait_send()

    @when(relay)
    def _():
        for i in (0, 1):
            for leg in (0, 1):
                crossing(ra, rm, rc, cs, cr, i, leg).wait_send()
                crossing(ba, bm, bc, bcs, bcr, i, leg).wait_send()

        @when(serves)
        def _():
            kv_final().wait_send()

        @when(goes, y < ny - 1)
        def _():
            back_final().wait_send()

    def drain(j, carry):
        for r in range(CHUNKS):

            @when(j <= h, h < nz - 1)
            def _():
                send_enc_right(j, r).wait_send()

            @when(j >= h, h > 0)
            def _():
                send_enc_left(j, r).wait_send()

            @when(j > h)
            def _():
                sum_right(j, r).wait_send()

            @when(j < h)
            def _():
                sum_left(j, r).wait_send()

        return carry

    lax.fori_loop(0, nz, drain, 0)


def shards(nz, queries, encodings, key_weight, value_weight, text_length, image_offset, cotangent):
    nx, nh, ny, nc = GRID
    tokens, width = queries.shape
    _, lmax, feat = encodings.shape
    depth = key_weight.shape[0]
    assert nx * nh == nz and ny * nc * depth == feat
    piece = lmax // ny
    dma = pltpu.SemaphoreType.DMA
    vmem = pl.BlockSpec(memory_space=pltpu.VMEM)
    smem = pl.BlockSpec(memory_space=pltpu.SMEM)
    part = pltpu.VMEM((piece, 2 * width), BF)
    whole = pltpu.VMEM((lmax, 2 * width), BF)
    far = max(nx, ny) - 1
    scratch = [
        pltpu.VMEM((nx, nh, ny, nc, depth, 2 * width), BF),
        pltpu.VMEM((depth, 2 * width), BF),
        pltpu.VMEM((nz, lmax, feat), BF),
        pltpu.VMEM((2, lmax, 2 * width), BF),
        pltpu.VMEM((2, 8, lmax), F32),
        part, part, part, part, part, part,
        pltpu.VMEM((lmax, 2 * width), F32),
        whole, whole, whole,
        pltpu.VMEM((nz, lmax, feat), BF),
        pltpu.VMEM((nz, lmax, feat), BF),
        pltpu.VMEM((lmax, 2 * width), F32),
        dma((2, far, nh)), dma((2, far, nh)), dma((2, far, nh)), dma((2, far, nh)),
        dma((4,)), dma((4,)), dma((nh,)), dma((nh,)),
        dma((nz, CHUNKS)), dma((nz, CHUNKS)), dma((nz, CHUNKS)), dma((nz, CHUNKS)),
        dma((1,)), dma((1,)),
        dma((1,)), dma((1,)), dma((ny,)), dma((1,)), dma((2, 2)), dma((2, 2)), dma((1,)), dma((ny,)),
        dma((1,)), dma((1,)), dma((ny,)), dma((1,)), dma((2, 2)), dma((2, 2)), dma((1,)), dma((ny,)),
        dma((nz, CHUNKS)), dma((nz, CHUNKS)), dma((nz, CHUNKS)), dma((nz, CHUNKS)),
    ]
    return pl.pallas_call(
        functools.partial(kernel, (nx, nh, ny, nc, nz)),
        out_shape=(
            jax.ShapeDtypeStruct(queries.shape, BF),
            jax.ShapeDtypeStruct(queries.shape, BF),
            jax.ShapeDtypeStruct(encodings.shape, BF),
        ),
        in_specs=[smem, smem] + [vmem] * 5,
        out_specs=(vmem, vmem, vmem),
        scratch_shapes=scratch,
        compiler_params=pltpu.CompilerParams(
            collective_id=0, has_side_effects=True, vmem_limit_bytes=56 * 2**20
        ),
        name="flow_block",
    )(text_length, image_offset, queries, cotangent, encodings, key_weight, value_weight)


def solution(mesh):
    return jax.shard_map(
        functools.partial(shards, mesh.shape["head"]),
        mesh=mesh,
        in_specs=(
            P("seq", "head"),
            P("seq", None, "head"),
            P("seq", "head"),
            P("seq", "head"),
            P("seq"),
            P("seq"),
            P("seq", "head"),
        ),
        out_specs=(P("seq", "head"), P("seq", "head"), P("seq", None, "head")),
        check_vma=False,
    )
```

```python
import functools
import math

import jax
import jax.numpy as jnp
from jax import lax
from jax.experimental import pallas as pl
from jax.experimental.pallas import tpu as pltpu
from jax.sharding import PartitionSpec as P

HD = 128
GRID = (4, 2, 4, 2)
CHUNKS = 4
BF = jnp.bfloat16
F32 = jnp.float32
MESH = pl.DeviceIdType.MESH


def dot(a, b, da, db):
    return lax.dot_general(a, b, (((da,), (db,)), ((), ())), preferred_element_type=F32)


def kernel(
    dims, len_ref, off_ref, q_ref, g_ref, enc_ref, wk_ref, wv_ref,
    out_ref, dq_ref, de_ref,
    w, wmid, enc, kv, qg, qp, ro, rn, rp, ra, rm, rc, ba, bm, bc, dkv32, dkv, rr, rl, parts,
    wss, wrs, wsx, wrx, wsb, wrb, wso, wro, gate,
    esr, err, esl, erl,
    ks, kr, ps, pr, cs, cr, fs, fr,
    bks, bkr, bps, bpr, bcs, bcr, bfs, bfr,
    rsr, rrr, rsl, rrl,
):
    nx, nh, ny, nc, nz = dims
    width = wk_ref.shape[1]
    heads = width // HD
    lmax = enc_ref.shape[1]
    tokens = q_ref.shape[0]
    piece = tokens // ny
    rows = lmax // CHUNKS
    s = lax.axis_index("seq")
    h = lax.axis_index("head")
    c = s % nc
    y = (s // nc) % ny
    zh = (s // (nc * ny)) % nh
    x = s // (nc * ny * nh)
    last = nx * nh * ny * nc - 1

    def at(x_, zh_, y_, c_):
        return ((x_ * nh + zh_) * ny + y_) * nc + c_

    def along(steps):
        z = (zh * nz + h + steps + nh * nz) % (nh * nz)
        return (at(x, z // nz, y, c), z % nz), z // nz

    sib = (at(x, zh, y, 1 - c), h)
    up, zh_up = along(nz // 2)
    down, zh_down = along(-(nz // 2))
    place = ((x, nx), (y, ny))

    def beside(axis, way):
        here, size = place[axis]
        there = (here + way + size) % size
        return there, ((at(there, zh, y, c) if axis == 0 else at(x, zh, there, c)), h)

    right = (s, h + 1)
    left = (s, h - 1)
    KC, VC = slice(0, width), slice(width, 2 * width)

    has_next = s < last
    has_prev = s > 0
    far_next = jnp.logical_and(c == nc - 1, y == ny - 1)
    far_prev = jnp.logical_and(c == 0, y == 0)
    near_next = jnp.logical_and(c == nc - 1, y < ny - 1)
    near_prev = jnp.logical_and(c == 0, y > 0)
    first_core = c == 0
    second_core = c == nc - 1
    serves = jnp.logical_or(zh == 1, x < nx - 1)
    served = (at(jnp.where(zh == 1, x, x + 1), zh, 0, 0), h)
    itself = jnp.logical_and(zh == 1, jnp.logical_and(first_core, y == 0))
    goes = jnp.logical_not(jnp.logical_and(zh == 1, x == nx - 1))
    source = (at(x, zh, ny - 1, nc - 1), h)
    source_x = jnp.where(zh == 1, x, x - 1)

    def when(*conds):
        return pl.when(functools.reduce(jnp.logical_and, conds))

    def copy(src, dst, ss, rs, dev):
        return pltpu.make_async_remote_copy(
            src_ref=src, dst_ref=dst, send_sem=ss, recv_sem=rs, device_id=dev, device_id_type=MESH
        )

    barrier = pltpu.get_barrier_semaphore()

    def hello(dev):
        pl.semaphore_signal(barrier, inc=1, device_id=dev, device_id_type=MESH)

    hello(sib)
    hello(up)
    hello(down)

    @when(h < nz - 1)
    def _():
        hello(right)

    @when(h > 0)
    def _():
        hello(left)

    @when(near_next)
    def _():
        hello((s + 1, h))

    @when(near_prev)
    def _():
        hello((s - 1, h))

    @when(first_core)
    def _():
        for axis in (0, 1):
            for way in (1, -1):
                hello(beside(axis, way)[1])

    @when(serves, jnp.logical_not(itself))
    def _():
        hello(served)

    beside_source = jnp.logical_and(goes, jnp.logical_not(far_next))

    @when(beside_source)
    def _():
        hello(source)

    far_target = jnp.logical_and(far_prev, has_prev)
    far_source = jnp.logical_and(far_next, has_next)

    @when(far_target)
    def _():
        for i in range(ny):
            hello((at(source_x, zh, i, nc - 1), h))
            if i > 0:
                hello((at(source_x, zh, i, 0), h))

        @when(zh == 0)
        def _():
            hello((at(source_x, zh, 0, 0), h))

    @when(far_source)
    def _():
        for i in range(ny):
            hello((at(x, zh, i, 0), h))
            if i < ny - 1:
                hello((at(x, zh, i, nc - 1), h))

    @when(first_core)
    def _():
        w[x, zh, y, 0, :, KC] = wk_ref[...]
        w[x, zh, y, 0, :, VC] = wv_ref[...]

    @when(second_core)
    def _():
        wmid[0, :, KC] = wk_ref[...]
        wmid[0, :, VC] = wv_ref[...]

    enc[h] = enc_ref[0]
    own = lax.broadcasted_iota(jnp.int32, (tokens, width), 0) >= off_ref[0]
    for cols, ref in ((KC, q_ref), (VC, g_ref)):
        block = ref[...].astype(F32)
        qg[1, :, cols] = jnp.where(own, block, 0.0).astype(BF)
        qp[:, cols] = jnp.where(own, 0.0, block).astype(BF)

    @when(s == 0)
    def _():
        rp[...] = jnp.zeros_like(rp)

    @when(s == last)
    def _():
        qg[0] = jnp.zeros((tokens, 2 * width), BF)

    @when(h == 0)
    def _():
        rr[...] = jnp.zeros_like(rr)

    @when(h == nz - 1)
    def _():
        rl[...] = jnp.zeros_like(rl)

    @when(first_core, jnp.logical_not(serves))
    def _():
        ba[...] = jnp.zeros_like(ba)

    @when(second_core, jnp.logical_not(goes))
    def _():
        ra[...] = jnp.zeros_like(ra)

    def n(flag):
        return flag.astype(jnp.int32)

    count = 3 + n(h < nz - 1) + n(h > 0) + n(near_next) + n(near_prev) + 4 * n(first_core)
    count = count + n(jnp.logical_and(serves, jnp.logical_not(itself))) + n(beside_source)
    count = count + n(far_target) * (2 * ny - 1 + n(zh == 0)) + n(far_source) * (2 * ny - 1)
    pl.semaphore_wait(barrier, count)

    def lend():
        return copy(wmid.at[0], w.at[x, zh, y, nc - 1], wso.at[0], wro.at[0], sib)

    def cross(i, leg):
        cols, dev, z_ = (KC, up, zh_down) if i == 0 else (VC, down, zh_up)
        mid = wmid.at[:, :, cols]
        if leg == 0:
            return copy(w.at[x, zh, y, :, :, cols], mid, wsx.at[2 * i], wrx.at[2 * i], dev)
        return copy(mid, w.at[x, z_, y, :, :, cols], wsx.at[2 * i + 1], wrx.at[2 * i + 1], dev)

    def hop(stage, which, z_, k):
        axis = which if stage == 0 else 1 - which
        index = place[axis][0] if k < 2 else beside(axis, -1 if k == 2 else 1)[0]
        dev = beside(axis, 1 if k % 2 == 0 else -1)[1]
        cols = KC if which == 0 else VC
        core = slice(None) if k < 2 else k - 2
        if axis == 0:
            ref = w.at[index, z_, y, core, :, cols] if stage == 0 else w.at[index, z_, :, core, :, cols]
        else:
            ref = w.at[x, z_, index, core, :, cols] if stage == 0 else w.at[:, z_, index, core, :, cols]
        return copy(ref, ref, wss.at[stage, which, z_, k], wrs.at[stage, which, z_, k], dev)

    def share(which, z_, d):
        here, size = place[1 - which]
        index = (here + d) % size
        ref = w.at[:, z_, index, :, :, KC] if which == 0 else w.at[index, z_, :, :, :, VC]
        return copy(ref, ref, wsb.at[which, z_, d], wrb.at[which, z_, d], sib)

    def send(stage, z_, ks_):
        for which in (0, 1):
            for k in ks_:
                hop(stage, which, z_, k).start()

    def receive(stage, z_, ks_):
        for which in (0, 1):
            for k in ks_:
                hop(stage, which, z_, k).wait_recv()

    def shares(z_, ds, act):
        for which in (0, 1):
            for d in ds:
                act(share(which, z_, d))

    def start(cp):
        cp.start()

    other = 1 - zh

    def task_a():
        lend().wait_recv()
        for i in (0, 1):
            cross(i, 0).start()
        send(0, zh, (0, 1))

    def task_b():
        receive(0, zh, (0, 1))
        send(0, zh, (2, 3))

    def task_c():
        for i in (0, 1):
            cross(i, 0).wait_recv()
            cross(i, 1).start()

    def task_d():
        receive(0, zh, (2, 3))
        send(1, zh, (0, 1))

    def task_e():
        for i in (0, 1):
            cross(i, 1).wait_recv()
        send(0, other, (0, 1))

    def task_f():
        receive(0, other, (0, 1))
        send(0, other, (2, 3))

    def task_g():
        receive(1, zh, (0, 1))
        send(1, zh, (2, 3))
        shares(zh, (0, 1, 3), start)

    def task_h():
        receive(0, other, (2, 3))
        send(1, other, (0, 1))

    def task_i():
        receive(1, zh, (2, 3))
        shares(zh, (2,), start)

    def task_j():
        receive(1, other, (0, 1))
        send(1, other, (2, 3))
        shares(other, (0, 1, 3), start)

    def task_k():
        receive(1, other, (2, 3))
        shares(other, (2,), start)

    def crossing(src, mid, dst, ss, rs, i, leg):
        cols, dev = (KC, up) if i == 0 else (VC, down)
        a, b = (src, mid) if leg == 0 else (mid, dst)
        return copy(a.at[:, cols], b.at[:, cols], ss.at[i, leg], rs.at[i, leg], dev)

    def back_crossing(i, leg):
        return crossing(ba, bm, bc, bcs, bcr, i, leg)

    def there_crossing(i, leg):
        return crossing(ra, rm, rc, cs, cr, i, leg)

    def back_direct():
        return copy(qp, qg.at[0], bks.at[0], bkr.at[0], (s - 1, h))

    def back_part(i):
        return copy(qp.at[pl.ds(i * piece, piece)], ba, bps.at[i], bpr.at[0], (at(source_x, zh, i, 0), h))

    def back_final(i):
        return copy(bc, qg.at[0, pl.ds(i * piece, piece)], bfs.at[0], bfr.at[i], source)

    def back_start():
        @when(has_prev, jnp.logical_not(far_prev))
        def _():
            back_direct().start()

        @when(far_target)
        def _():
            for i in range(1, ny):
                back_part(i).start()

            @when(zh == 0)
            def _():
                back_part(0).start()

            @when(zh == 1)
            def _():
                ba[...] = qp[:piece, :]

    def back_one():
        @when(serves, jnp.logical_not(itself))
        def _():
            back_part(0).wait_recv()

        for i in (0, 1):
            back_crossing(i, 0).start()

    def back_two():
        for i in (0, 1):
            back_crossing(i, 0).wait_recv()
            back_crossing(i, 1).start()

    def back_three():
        for i in (0, 1):
            back_crossing(i, 1).wait_recv()
        for i in range(ny):

            @when(goes, y == i)
            def _():
                back_final(i).start()

    def back_arrived():
        @when(has_next)
        def _():
            @when(jnp.logical_not(far_next))
            def _():
                back_direct().wait_recv()

            @when(far_next)
            def _():
                for i in range(ny):
                    back_final(i).wait_recv()

    def send_enc_right(j, r):
        ref = enc.at[j, pl.ds(r * rows, rows)]
        return copy(ref, ref, esr.at[j, r], err.at[j, r], right)

    def send_enc_left(j, r):
        ref = enc.at[j, pl.ds(r * rows, rows)]
        return copy(ref, ref, esl.at[j, r], erl.at[j, r], left)

    def project(f):
        if nx * nh == nz:
            block = w[f // nh, f % nh].reshape(-1, 2 * width)
        else:
            block = w[f].reshape(-1, 2 * width)
        return dot(enc[f], block, 1, 0)

    def gather(todo, projecting):
        for st in range(nz):
            for r in range(CHUNKS):
                if st > 0:

                    @when(h - st >= 0)
                    def _():
                        send_enc_right(h - st, r).wait_recv()

                if st < nz - 1:

                    @when(h - st >= 0, h < nz - 1)
                    def _():
                        send_enc_right(h - st, r).start()

                if st > 0:

                    @when(h + st < nz)
                    def _():
                        send_enc_left(h + st, r).wait_recv()

                if st < nz - 1:

                    @when(h + st < nz, h > 0)
                    def _():
                        send_enc_left(h + st, r).start()

            for task in todo.get(st, ()):
                task()
            if projecting:
                for d in {nz - 4: (0, 1), nz - 3: (2, 3), nz - 2: (4, 5), nz - 1: (6, 7)}.get(st, ()):
                    if d == 0:
                        dkv32[...] = project(h)
                    else:

                        @when(h - d >= 0)
                        def _():
                            dkv32[...] += project(h - d)

                        @when(h + d < nz)
                        def _():
                            dkv32[...] += project(h + d)

    back_start()

    @when(second_core)
    def _():
        lend().start()
        gather({}, False)
        pl.semaphore_signal(gate, inc=1, device_id=sib, device_id_type=MESH)
        for z_ in (0, 1):
            for which in (0, 1):
                for d in range(4):
                    share(which, z_, d).wait_recv()
        dkv32[...] = jnp.zeros_like(dkv32)

        def one(f, carry):
            dkv32[...] += project(f)
            return carry

        lax.fori_loop(0, nz, one, 0)

    @when(first_core)
    def _():
        for task in (
            task_a, task_b, back_one, task_c, task_d, task_e, back_two, task_f, task_g, task_h, task_i, back_three,
        ):
            task()
        pl.semaphore_wait(gate, 1)
        gather({1: (task_j,), 2: (task_k,)}, True)

    kv[...] = dkv32[...].astype(BF)

    scale = 1.0 / math.sqrt(HD)
    ok = lax.broadcasted_iota(jnp.int32, (1, lmax), 1) < len_ref[0]
    for b in (1, 0):
        if b == 0:
            back_arrived()
        result = ro if b == 1 else rn
        for a in range(heads):
            kc = slice(a * HD, (a + 1) * HD)
            vc = slice(width + a * HD, width + (a + 1) * HD)
            q = qg[b, :, kc]
            g = qg[b, :, vc]
            k = kv[:, kc]
            v = kv[:, vc]
            scores = jnp.where(ok, dot(q, k, 1, 1) * scale, -1e30)
            expo = jnp.exp(scores - jnp.max(scores, axis=-1, keepdims=True))
            probs = expo / jnp.sum(expo, axis=-1, keepdims=True)
            dprobs = dot(g, v, 1, 1)
            delta = jnp.sum(probs * dprobs, axis=-1, keepdims=True)
            ds = (probs * (dprobs - delta) * scale).astype(BF)
            pb = probs.astype(BF)
            result[:, kc] = dot(pb, v, 1, 0).astype(BF)
            result[:, vc] = dot(ds, k, 1, 0).astype(BF)
            dk = dot(ds, q, 0, 0)
            dv = dot(pb, g, 0, 0)
            if b == 1:
                dkv32[:, kc] = dk
                dkv32[:, vc] = dv
            else:
                dkv[:, kc] = (dkv32[:, kc] + dk).astype(BF)
                dkv[:, vc] = (dkv32[:, vc] + dv).astype(BF)

    def there_direct():
        return copy(rn, rp, ks.at[0], kr.at[0], (s + 1, h))

    def there_part(i):
        return copy(rn.at[pl.ds(i * piece, piece)], ra, ps.at[i], pr.at[0], (at(x, zh, i, nc - 1), h))

    def there_final(i):
        return copy(rc, rp.at[pl.ds(i * piece, piece)], fs.at[0], fr.at[i], served)

    def there_one():
        @when(goes, y < ny - 1)
        def _():
            there_part(0).wait_recv()

        for i in (0, 1):
            there_crossing(i, 0).start()

    def there_two():
        for i in (0, 1):
            there_crossing(i, 0).wait_recv()
            there_crossing(i, 1).start()

    def there_three():
        for i in (0, 1):
            there_crossing(i, 1).wait_recv()
        for i in range(ny):

            @when(serves, y == i)
            def _():
                there_final(i).start()

    @when(has_next, jnp.logical_not(far_next))
    def _():
        there_direct().start()

    @when(far_source)
    def _():
        for i in range(ny - 1):
            there_part(i).start()
        ra[...] = rn[(ny - 1) * piece :, :]

    def sum_right(j, r):
        ref = rr.at[j, pl.ds(r * rows, rows)]
        return copy(ref, ref, rsr.at[j, r], rrr.at[j, r], right)

    def sum_left(j, r):
        ref = rl.at[j, pl.ds(r * rows, rows)]
        return copy(ref, ref, rsl.at[j, r], rrl.at[j, r], left)

    def partial(j):
        if nx * nh == nz:
            block = w[j // nh, j % nh].reshape(-1, 2 * width)
        else:
            block = w[j].reshape(-1, 2 * width)
        return dot(dkv[...], block, 1, 1)

    def reduce_step(t, carry):
        going_right = jnp.logical_and(t >= h, h < nz - 1)
        going_left = jnp.logical_and(t >= nz - 1 - h, h > 0)
        jr = nz - 1 + h - t
        jl = t - (nz - 1 - h)

        @when(going_right)
        def _():
            parts[0] = partial(jr)

        @when(going_left)
        def _():
            parts[1] = partial(jl)

        for r in range(CHUNKS):
            here = pl.ds(r * rows, rows)

            @when(going_right)
            def _():
                @when(h > 0)
                def _():
                    sum_right(jr, r).wait_recv()

                rr[jr, here, :] = (parts[0, here, :] + rr[jr, here, :].astype(F32)).astype(BF)
                sum_right(jr, r).start()

            @when(going_left)
            def _():
                @when(h < nz - 1)
                def _():
                    sum_left(jl, r).wait_recv()

                rl[jl, here, :] = (parts[1, here, :] + rl[jl, here, :].astype(F32)).astype(BF)
                sum_left(jl, r).start()

        @when(second_core, t == nz // 2)
        def _():
            there_one()

        return carry

    lax.fori_loop(0, nz - 1, reduce_step, 0)

    @when(second_core)
    def _():
        there_two()

    parts[0] = partial(h)
    for r in range(CHUNKS):
        here = pl.ds(r * rows, rows)

        @when(h > 0)
        def _():
            sum_right(h, r).wait_recv()

        @when(h < nz - 1)
        def _():
            sum_left(h, r).wait_recv()

        total = parts[0, here, :] + rr[h, here, :].astype(F32) + rl[h, here, :].astype(F32)
        de_ref[0, here, :] = total.astype(BF)

    @when(second_core)
    def _():
        there_three()

    @when(has_prev)
    def _():
        @when(jnp.logical_not(far_prev))
        def _():
            there_direct().wait_recv()

        @when(far_prev)
        def _():
            for i in range(ny):
                there_final(i).wait_recv()

    own = lax.broadcasted_iota(jnp.int32, (tokens, width), 0) >= off_ref[0]
    for cols, ref in ((KC, out_ref), (VC, dq_ref)):
        ref[...] = jnp.where(own, ro[:, cols].astype(F32), rp[:, cols].astype(F32)).astype(BF)

    @when(first_core)
    def _():
        for z_ in (0, 1):
            for which in (0, 1):
                for d in range(4):
                    share(which, z_, d).wait_send()
                    for stage in (0, 1):
                        hop(stage, which, z_, d).wait_send()
        for i in (0, 1):
            for leg in (0, 1):
                cross(i, leg).wait_send()
                back_crossing(i, leg).wait_send()

        @when(goes)
        def _():
            back_final(0).wait_send()

    @when(second_core)
    def _():
        lend().wait_send()
        for i in (0, 1):
            for leg in (0, 1):
                there_crossing(i, leg).wait_send()

        @when(serves)
        def _():
            there_final(0).wait_send()

    @when(has_prev, jnp.logical_not(far_prev))
    def _():
        back_direct().wait_send()

    @when(far_target)
    def _():
        for i in range(1, ny):
            back_part(i).wait_send()

        @when(zh == 0)
        def _():
            back_part(0).wait_send()

    @when(has_next, jnp.logical_not(far_next))
    def _():
        there_direct().wait_send()

    @when(far_source)
    def _():
        for i in range(ny - 1):
            there_part(i).wait_send()

    def drain(j, carry):
        for r in range(CHUNKS):

            @when(j <= h, h < nz - 1)
            def _():
                send_enc_right(j, r).wait_send()

            @when(j >= h, h > 0)
            def _():
                send_enc_left(j, r).wait_send()

            @when(j > h)
            def _():
                sum_right(j, r).wait_send()

            @when(j < h)
            def _():
                sum_left(j, r).wait_send()

        return carry

    lax.fori_loop(0, nz, drain, 0)


def shards(nz, queries, encodings, key_weight, value_weight, text_length, image_offset, cotangent):
    nx, nh, ny, nc = GRID
    tokens, width = queries.shape
    _, lmax, feat = encodings.shape
    depth = key_weight.shape[0]
    assert ny * nc * depth * nx * nh == feat * nz
    dma = pltpu.SemaphoreType.DMA
    vmem = pl.BlockSpec(memory_space=pltpu.VMEM)
    smem = pl.BlockSpec(memory_space=pltpu.SMEM)
    block = pltpu.VMEM((tokens, 2 * width), BF)
    part = pltpu.VMEM((tokens // ny, 2 * width), BF)
    line = dma((nz, CHUNKS))
    scratch = [
        pltpu.VMEM((nx, nh, ny, nc, depth, 2 * width), BF),
        pltpu.VMEM((nc, depth, 2 * width), BF),
        pltpu.VMEM((nz, lmax, feat), BF),
        pltpu.VMEM((lmax, 2 * width), BF),
        pltpu.VMEM((2, tokens, 2 * width), BF),
        block, block, block, block,
        part, part, part, part, part, part,
        pltpu.VMEM((lmax, 2 * width), F32),
        pltpu.VMEM((lmax, 2 * width), BF),
        pltpu.VMEM((nz, lmax, feat), BF),
        pltpu.VMEM((nz, lmax, feat), BF),
        pltpu.VMEM((2, lmax, feat), F32),
        dma((2, 2, nh, 4)), dma((2, 2, nh, 4)), dma((4,)), dma((4,)), dma((2, nh, 4)), dma((2, nh, 4)), dma((1,)), dma((1,)),
        pltpu.SemaphoreType.REGULAR,
        line, line, line, line,
        dma((1,)), dma((1,)), dma((ny,)), dma((1,)), dma((2, 2)), dma((2, 2)), dma((1,)), dma((ny,)),
        dma((1,)), dma((1,)), dma((ny,)), dma((1,)), dma((2, 2)), dma((2, 2)), dma((1,)), dma((ny,)),
        line, line, line, line,
    ]
    return pl.pallas_call(
        functools.partial(kernel, (nx, nh, ny, nc, nz)),
        out_shape=(
            jax.ShapeDtypeStruct(queries.shape, BF),
            jax.ShapeDtypeStruct(queries.shape, BF),
            jax.ShapeDtypeStruct(encodings.shape, BF),
        ),
        in_specs=[smem, smem] + [vmem] * 5,
        out_specs=(vmem, vmem, vmem),
        scratch_shapes=scratch,
        compiler_params=pltpu.CompilerParams(
            collective_id=0, has_side_effects=True, vmem_limit_bytes=56 * 2**20
        ),
        name="flow_block",
    )(text_length, image_offset, queries, cotangent, encodings, key_weight, value_weight)


def solution(mesh):
    return jax.shard_map(
        functools.partial(shards, mesh.shape["head"]),
        mesh=mesh,
        in_specs=(
            P("seq", "head"),
            P("seq", None, "head"),
            P("seq", "head"),
            P("seq", "head"),
            P("seq"),
            P("seq"),
            P("seq", "head"),
        ),
        out_specs=(P("seq", "head"), P("seq", "head"), P("seq", None, "head")),
        check_vma=False,
    )
```

```python
import functools
import math

import jax
import jax.numpy as jnp
from jax import lax
from jax.experimental import pallas as pl
from jax.experimental.pallas import tpu as pltpu
from jax.sharding import PartitionSpec as P

HD = 128
GRID = (4, 2, 4, 2)
CHUNKS = 4
GATE = 7
BF = jnp.bfloat16
F32 = jnp.float32
MESH = pl.DeviceIdType.MESH


def dot(a, b, da, db):
    return lax.dot_general(a, b, (((da,), (db,)), ((), ())), preferred_element_type=F32)


def kernel(
    dims, len_ref, off_ref, q_ref, g_ref, enc_ref, wk_ref, wv_ref,
    out_ref, dq_ref, de_ref,
    w, mine, wmid, enc, kv, qg, qp, ro, rn, rp, ra, rm, rc, ba, bm, bc, dkv32, dkv, rr, rl, parts,
    wss, wrs, wts, wtr, wsx, wrx, wsb, wrb, wso, wro, gate,
    esr, err, esl, erl,
    ks, kr, ps, pr, cs, cr, fs, fr,
    bks, bkr, bps, bpr, bcs, bcr, bfs, bfr,
    rsr, rrr, rsl, rrl,
):
    nx, nh, ny, nc, nz = dims
    width = wk_ref.shape[1]
    heads = width // HD
    lmax = enc_ref.shape[1]
    tokens = q_ref.shape[0]
    piece = tokens // ny
    rows = lmax // CHUNKS
    s = lax.axis_index("seq")
    h = lax.axis_index("head")
    c = s % nc
    y = (s // nc) % ny
    zh = (s // (nc * ny)) % nh
    x = s // (nc * ny * nh)
    last = nx * nh * ny * nc - 1

    def at(x_, zh_, y_, c_):
        return ((x_ * nh + zh_) * ny + y_) * nc + c_

    def along(steps):
        z = (zh * nz + h + steps + nh * nz) % (nh * nz)
        return (at(x, z // nz, y, c), z % nz), z // nz

    sib = (at(x, zh, y, 1 - c), h)
    up, zh_up = along(nz // 2)
    down, zh_down = along(-(nz // 2))
    place = ((x, nx), (y, ny))

    def beside(axis, way):
        here, size = place[axis]
        there = (here + way + size) % size
        return there, ((at(there, zh, y, c) if axis == 0 else at(x, zh, there, c)), h)

    right = (s, h + 1)
    left = (s, h - 1)
    KC, VC = slice(0, width), slice(width, 2 * width)

    has_next = s < last
    has_prev = s > 0
    far_next = jnp.logical_and(c == nc - 1, y == ny - 1)
    far_prev = jnp.logical_and(c == 0, y == 0)
    near_next = jnp.logical_and(c == nc - 1, y < ny - 1)
    near_prev = jnp.logical_and(c == 0, y > 0)
    first_core = c == 0
    second_core = c == nc - 1
    serves = jnp.logical_and(second_core, jnp.logical_or(zh == 1, x < nx - 1))
    served = (at(jnp.where(zh == 1, x, x + 1), zh, 0, 0), h)
    goes = jnp.logical_and(second_core, jnp.logical_not(jnp.logical_and(zh == 1, x == nx - 1)))
    source = (at(x, zh, ny - 1, nc - 1), h)
    source_x = jnp.where(zh == 1, x, x - 1)

    def when(*conds):
        return pl.when(functools.reduce(jnp.logical_and, conds))

    def copy(src, dst, ss, rs, dev):
        return pltpu.make_async_remote_copy(
            src_ref=src, dst_ref=dst, send_sem=ss, recv_sem=rs, device_id=dev, device_id_type=MESH
        )

    barrier = pltpu.get_barrier_semaphore()

    def hello(dev):
        pl.semaphore_signal(barrier, inc=1, device_id=dev, device_id_type=MESH)

    hello(sib)
    for dev in (up, down):
        hello(dev)
        hello((dev[0] + 1 - 2 * c, dev[1]))

    @when(h < nz - 1)
    def _():
        hello(right)

    @when(h > 0)
    def _():
        hello(left)

    @when(near_next)
    def _():
        hello((s + 1, h))

    @when(near_prev)
    def _():
        hello((s - 1, h))

    for axis in (0, 1):
        for way in (1, -1):
            hello(beside(axis, way)[1])

    beside_source = jnp.logical_and(goes, y < ny - 1)
    far_target = jnp.logical_and(far_prev, has_prev)
    far_source = jnp.logical_and(far_next, has_next)

    @when(serves)
    def _():
        hello(served)

    @when(beside_source)
    def _():
        hello(source)

    @when(far_target)
    def _():
        for i in range(ny):
            hello((at(source_x, zh, i, nc - 1), h))

    @when(far_source)
    def _():
        for i in range(ny - 1):
            hello((at(x, zh, i, nc - 1), h))

    mine[:, KC] = wk_ref[...]
    mine[:, VC] = wv_ref[...]

    @when(first_core)
    def _():
        w[x, zh, y, 0, :, KC] = wk_ref[...]

    @when(second_core)
    def _():
        w[x, zh, y, nc - 1, :, VC] = wv_ref[...]

    enc[h] = enc_ref[0]

    @when(s == 0)
    def _():
        rp[...] = jnp.zeros_like(rp)

    @when(s == last)
    def _():
        qg[0] = jnp.zeros((tokens, 2 * width), BF)

    @when(h == 0)
    def _():
        rr[...] = jnp.zeros_like(rr)

    @when(h == nz - 1)
    def _():
        rl[...] = jnp.zeros_like(rl)

    @when(second_core, jnp.logical_not(serves))
    def _():
        ba[...] = jnp.zeros_like(ba)

    @when(second_core, jnp.logical_not(goes))
    def _():
        ra[...] = jnp.zeros_like(ra)

    def n(flag):
        return flag.astype(jnp.int32)

    count = 9 + n(h < nz - 1) + n(h > 0) + n(near_next) + n(near_prev) + n(serves) + n(beside_source)
    count = count + ny * n(far_target) + (ny - 1) * n(far_source)
    pl.semaphore_wait(barrier, count)

    def lend(i):
        cols = KC if i == 0 else VC
        return copy(mine.at[:, cols], w.at[x, zh, y, 1 - i, :, cols], wso.at[i], wro.at[i], sib)

    def cross(i, leg):
        cols, dev, z_ = (KC, up, zh_down) if i == 0 else (VC, down, zh_up)
        if leg == 0:
            return copy(mine.at[:, cols], wmid.at[:, cols], wsx.at[i, 0], wrx.at[i, 0, 0], dev)
        return copy(wmid.at[:, cols], w.at[x, z_, y, c, :, cols], wsx.at[i, 1], wrx.at[i, 1, c], (dev[0] - c + i, dev[1]))

    def cross_mid():
        for i in (0, 1):
            cross(i, 0).wait_recv()
            cross(i, 1).start()

    def cross_arrived(i):
        cols = KC if i == 0 else VC
        for core in range(nc):
            ref = w.at[x, 1 - zh, y, core, :, cols]
            copy(wmid.at[:, cols], ref, wsx.at[i, 1], wrx.at[i, 1, core], sib).wait_recv()

    def block_of(which, stage, z_, index, e, core):
        cols = KC if which == 0 else VC
        along_x = which == stage
        across = e if stage == 0 or isinstance(e, slice) else (place[which][0] + e) % place[which][1]
        if stage == 0:
            return w.at[index, z_, y, core, :, cols] if along_x else w.at[x, z_, index, core, :, cols]
        return w.at[index, z_, across, core, :, cols] if along_x else w.at[across, z_, index, core, :, cols]

    whole = slice(None)

    def hop(stage, which, z_, k):
        axis = which if stage == 0 else 1 - which
        index = place[axis][0] if k < 2 else beside(axis, -1 if k == 2 else 1)[0]
        dev = beside(axis, 1 if k % 2 == 0 else -1)[1]
        ref = block_of(which, stage, z_, index, whole, whole if k < 2 else k - 2)
        return copy(ref, ref, wss.at[stage, which, z_, k], wrs.at[stage, which, z_, k], dev)

    def second(which, z_, k, e):
        axis = 1 - which
        ref = block_of(which, 1, z_, place[axis][0], e, whole)
        dev = beside(axis, 1 if k == 0 else -1)[1]
        return copy(ref, ref, wts.at[which, z_, k, e], wtr.at[which, z_, k, e], dev)

    def seconds(which, z_, es, act):
        for e in es:
            for k in (0, 1):
                act(second(which, z_, k, e))

    def share(which, z_, d):
        here, size = place[1 - which]
        index = (here + d) % size
        ref = w.at[:, z_, index, :, :, KC] if which == 0 else w.at[index, z_, :, :, :, VC]
        return copy(ref, ref, wsb.at[which, z_, d], wrb.at[which, z_, d], sib)

    def start(cp):
        cp.start()

    def arrived(cp):
        cp.wait_recv()

    def gone(cp):
        cp.wait_send()

    def firsts(which, z_, ks_, act):
        for k in ks_:
            act(hop(0, which, z_, k))

    def lasts(which, z_, act):
        for k in (2, 3):
            act(hop(1, which, z_, k))

    def shares(which, z_, ds, act):
        for d in ds:
            act(share(which, z_, d))

    other = 1 - zh

    def spread(which):
        def one(z_):
            firsts(which, z_, (0, 1), start)
            seconds(which, z_, (0,), start)

        def two(z_):
            firsts(which, z_, (0, 1), arrived)
            firsts(which, z_, (2, 3), start)
            seconds(which, z_, (1, 3), start)

        def three(z_):
            firsts(which, z_, (2, 3), arrived)
            seconds(which, z_, (2,), start)

        def four(z_):
            seconds(which, z_, range(4), arrived)
            lasts(which, z_, start)
            shares(which, z_, (0, 1, 3), start)

        def five(z_):
            lasts(which, z_, arrived)
            shares(which, z_, (2,), start)

        near = [functools.partial(f, zh) for f in (one, two, three, four, five)]
        near[0] = lambda: (lend(which).wait_recv(), one(zh))
        far = [functools.partial(f, other) for f in (one, two, three, four, five)]
        far[0] = lambda: (cross_arrived(which), one(other))
        return near, far

    def crossing(src, mid, dst, ss, rs, i, leg):
        cols, dev = (KC, up) if i == 0 else (VC, down)
        a, b = (src, mid) if leg == 0 else (mid, dst)
        return copy(a.at[:, cols], b.at[:, cols], ss.at[i, leg], rs.at[i, leg], dev)

    def back_crossing(i, leg):
        return crossing(ba, bm, bc, bcs, bcr, i, leg)

    def there_crossing(i, leg):
        return crossing(ra, rm, rc, cs, cr, i, leg)

    def back_direct():
        return copy(qp, qg.at[0], bks.at[0], bkr.at[0], (s - 1, h))

    def back_part(i):
        return copy(qp.at[pl.ds(i * piece, piece)], ba, bps.at[i], bpr.at[0], (at(source_x, zh, i, nc - 1), h))

    def back_final(i):
        return copy(bc, qg.at[0, pl.ds(i * piece, piece)], bfs.at[0], bfr.at[i], source)

    def back_start():
        own = lax.broadcasted_iota(jnp.int32, (tokens, width), 0) >= off_ref[0]
        for cols, ref in ((KC, q_ref), (VC, g_ref)):
            block = ref[...].astype(F32)
            qg[1, :, cols] = jnp.where(own, block, 0.0).astype(BF)
            qp[:, cols] = jnp.where(own, 0.0, block).astype(BF)

        @when(has_prev, jnp.logical_not(far_prev))
        def _():
            back_direct().start()

        @when(far_target)
        def _():
            for i in range(ny):
                back_part(i).start()

    def back_one():
        @when(serves)
        def _():
            back_part(0).wait_recv()

        for i in (0, 1):
            back_crossing(i, 0).start()

    def back_two():
        for i in (0, 1):
            back_crossing(i, 0).wait_recv()
            back_crossing(i, 1).start()

    def back_three():
        for i in (0, 1):
            back_crossing(i, 1).wait_recv()
        for i in range(ny - 1):

            @when(goes, y == i)
            def _():
                back_final(i).start()

        @when(goes, y == ny - 1)
        def _():
            qg[0, (ny - 1) * piece :, :] = bc[...]

    def back_arrived():
        @when(has_next)
        def _():
            @when(jnp.logical_not(far_next))
            def _():
                back_direct().wait_recv()

            @when(far_next)
            def _():
                for i in range(ny - 1):
                    back_final(i).wait_recv()

    def send_enc_right(j, r):
        ref = enc.at[j, pl.ds(r * rows, rows)]
        return copy(ref, ref, esr.at[j, r], err.at[j, r], right)

    def send_enc_left(j, r):
        ref = enc.at[j, pl.ds(r * rows, rows)]
        return copy(ref, ref, esl.at[j, r], erl.at[j, r], left)

    def open_gate():
        pl.semaphore_signal(gate, inc=1, device_id=sib, device_id_type=MESH)

    def project(f):
        if nx * nh == nz:
            block = w[f // nh, f % nh].reshape(-1, 2 * width)
        else:
            block = w[f].reshape(-1, 2 * width)
        return dot(enc[f], block, 1, 0)

    def gather(todo, projecting):
        for st in range(nz):
            for r in range(CHUNKS):
                if st > 0:

                    @when(h - st >= 0)
                    def _():
                        send_enc_right(h - st, r).wait_recv()

                if st < nz - 1:

                    @when(h - st >= 0, h < nz - 1)
                    def _():
                        send_enc_right(h - st, r).start()

                if st > 0:

                    @when(h + st < nz)
                    def _():
                        send_enc_left(h + st, r).wait_recv()

                if st < nz - 1:

                    @when(h + st < nz, h > 0)
                    def _():
                        send_enc_left(h + st, r).start()

            for task in todo.get(st, ()):
                task()
            if projecting:
                for d in {nz - 4: (0, 1), nz - 3: (2, 3), nz - 2: (4, 5), nz - 1: (6, 7)}.get(st, ()):
                    if d == 0:
                        dkv32[...] = project(h)
                    else:

                        @when(h - d >= 0)
                        def _():
                            dkv32[...] += project(h - d)

                        @when(h + d < nz)
                        def _():
                            dkv32[...] += project(h + d)

    for i in (0, 1):
        cross(i, 0).start()

    @when(second_core)
    def _():
        lend(0).start()
        near, far = spread(1)
        gather(
            {
                0: (back_start, near[0]),
                1: (near[1], cross_mid),
                2: (near[2],),
                3: (near[3], back_one),
                4: (far[0], near[4]),
                5: (far[1],),
                6: (far[2], back_two),
                GATE: (open_gate,),
            },
            False,
        )
        far[3]()
        far[4]()
        back_three()
        dkv32[...] = jnp.zeros_like(dkv32)
        if nx * nh == nz:
            groups = ((zh, nh), (other, nh))
        else:
            groups = (None, (0, 1))
        for z_, group in zip((zh, other), groups):
            shares(0, z_, range(4), arrived)
            if group is not None:

                def one(f, carry):
                    dkv32[...] += project(group[0] + f * group[1])
                    return carry

                lax.fori_loop(0, nz // group[1], one, 0)

    @when(first_core)
    def _():
        lend(1).start()
        near, far = spread(0)
        for task in (
            near[0], back_start, near[1], cross_mid, near[2], near[3], far[0], near[4], far[1], far[2],
        ):
            task()
        pl.semaphore_wait(gate, 1)

        def whole_weights():
            for z_ in (0, 1):
                shares(1, z_, range(4), arrived)

        gather({0: (far[3],), 1: (far[4],), 3: (whole_weights,)}, True)

    kv[...] = dkv32[...].astype(BF)

    scale = 1.0 / math.sqrt(HD)
    ok = lax.broadcasted_iota(jnp.int32, (1, lmax), 1) < len_ref[0]
    for b in (1, 0):
        if b == 0:
            back_arrived()
        result = ro if b == 1 else rn
        for a in range(heads):
            kc = slice(a * HD, (a + 1) * HD)
            vc = slice(width + a * HD, width + (a + 1) * HD)
            q = qg[b, :, kc]
            g = qg[b, :, vc]
            k = kv[:, kc]
            v = kv[:, vc]
            scores = jnp.where(ok, dot(q, k, 1, 1) * scale, -1e30)
            expo = jnp.exp(scores - jnp.max(scores, axis=-1, keepdims=True))
            probs = expo / jnp.sum(expo, axis=-1, keepdims=True)
            dprobs = dot(g, v, 1, 1)
            delta = jnp.sum(probs * dprobs, axis=-1, keepdims=True)
            ds = (probs * (dprobs - delta) * scale).astype(BF)
            pb = probs.astype(BF)
            result[:, kc] = dot(pb, v, 1, 0).astype(BF)
            result[:, vc] = dot(ds, k, 1, 0).astype(BF)
            dk = dot(ds, q, 0, 0)
            dv = dot(pb, g, 0, 0)
            if b == 1:
                dkv32[:, kc] = dk
                dkv32[:, vc] = dv
            else:
                dkv[:, kc] = (dkv32[:, kc] + dk).astype(BF)
                dkv[:, vc] = (dkv32[:, vc] + dv).astype(BF)

    def there_direct():
        return copy(rn, rp, ks.at[0], kr.at[0], (s + 1, h))

    def there_part(i):
        return copy(rn.at[pl.ds(i * piece, piece)], ra, ps.at[i], pr.at[0], (at(x, zh, i, nc - 1), h))

    def there_final(i):
        return copy(rc, rp.at[pl.ds(i * piece, piece)], fs.at[0], fr.at[i], served)

    def there_one():
        @when(goes, y < ny - 1)
        def _():
            there_part(0).wait_recv()

        for i in (0, 1):
            there_crossing(i, 0).start()

    def there_two():
        for i in (0, 1):
            there_crossing(i, 0).wait_recv()
            there_crossing(i, 1).start()

    def there_three():
        for i in (0, 1):
            there_crossing(i, 1).wait_recv()
        for i in range(ny):

            @when(serves, y == i)
            def _():
                there_final(i).start()

    @when(has_next, jnp.logical_not(far_next))
    def _():
        there_direct().start()

    @when(far_source)
    def _():
        for i in range(ny - 1):
            there_part(i).start()
        ra[...] = rn[(ny - 1) * piece :, :]

    def sum_right(j, r):
        ref = rr.at[j, pl.ds(r * rows, rows)]
        return copy(ref, ref, rsr.at[j, r], rrr.at[j, r], right)

    def sum_left(j, r):
        ref = rl.at[j, pl.ds(r * rows, rows)]
        return copy(ref, ref, rsl.at[j, r], rrl.at[j, r], left)

    def partial(j):
        if nx * nh == nz:
            block = w[j // nh, j % nh].reshape(-1, 2 * width)
        else:
            block = w[j].reshape(-1, 2 * width)
        return dot(dkv[...], block, 1, 1)

    def reduce_step(t, carry):
        going_right = jnp.logical_and(t >= h, h < nz - 1)
        going_left = jnp.logical_and(t >= nz - 1 - h, h > 0)
        jr = nz - 1 + h - t
        jl = t - (nz - 1 - h)

        @when(going_right)
        def _():
            parts[0] = partial(jr)

        @when(going_left)
        def _():
            parts[1] = partial(jl)

        for r in range(CHUNKS):
            here = pl.ds(r * rows, rows)

            @when(going_right)
            def _():
                @when(h > 0)
                def _():
                    sum_right(jr, r).wait_recv()

                rr[jr, here, :] = (parts[0, here, :] + rr[jr, here, :].astype(F32)).astype(BF)
                sum_right(jr, r).start()

            @when(going_left)
            def _():
                @when(h < nz - 1)
                def _():
                    sum_left(jl, r).wait_recv()

                rl[jl, here, :] = (parts[1, here, :] + rl[jl, here, :].astype(F32)).astype(BF)
                sum_left(jl, r).start()

        @when(second_core, t == 1)
        def _():
            there_one()

        @when(second_core, t == 3)
        def _():
            there_two()

        @when(second_core, t == 5)
        def _():
            there_three()

        return carry

    lax.fori_loop(0, nz - 1, reduce_step, 0)

    parts[0] = partial(h)
    for r in range(CHUNKS):
        here = pl.ds(r * rows, rows)

        @when(h > 0)
        def _():
            sum_right(h, r).wait_recv()

        @when(h < nz - 1)
        def _():
            sum_left(h, r).wait_recv()

        total = parts[0, here, :] + rr[h, here, :].astype(F32) + rl[h, here, :].astype(F32)
        de_ref[0, here, :] = total.astype(BF)

    @when(has_prev)
    def _():
        @when(jnp.logical_not(far_prev))
        def _():
            there_direct().wait_recv()

        @when(far_prev)
        def _():
            for i in range(ny):
                there_final(i).wait_recv()

    own = lax.broadcasted_iota(jnp.int32, (tokens, width), 0) >= off_ref[0]
    for cols, ref in ((KC, out_ref), (VC, dq_ref)):
        ref[...] = jnp.where(own, ro[:, cols].astype(F32), rp[:, cols].astype(F32)).astype(BF)

    for i in (0, 1):
        for leg in (0, 1):
            cross(i, leg).wait_send()

    def weights_gone(which):
        lend(1 - which).wait_send()
        for z_ in (0, 1):
            shares(which, z_, range(4), gone)
            firsts(which, z_, range(4), gone)
            seconds(which, z_, range(4), gone)
            lasts(which, z_, gone)

    @when(first_core)
    def _():
        weights_gone(0)

    @when(second_core)
    def _():
        weights_gone(1)
        for i in (0, 1):
            for leg in (0, 1):
                back_crossing(i, leg).wait_send()
                there_crossing(i, leg).wait_send()

        @when(goes, y < ny - 1)
        def _():
            back_final(0).wait_send()

        @when(serves)
        def _():
            there_final(0).wait_send()

    @when(has_prev, jnp.logical_not(far_prev))
    def _():
        back_direct().wait_send()

    @when(far_target)
    def _():
        for i in range(ny):
            back_part(i).wait_send()

    @when(has_next, jnp.logical_not(far_next))
    def _():
        there_direct().wait_send()

    @when(far_source)
    def _():
        for i in range(ny - 1):
            there_part(i).wait_send()

    def drain(j, carry):
        for r in range(CHUNKS):

            @when(j <= h, h < nz - 1)
            def _():
                send_enc_right(j, r).wait_send()

            @when(j >= h, h > 0)
            def _():
                send_enc_left(j, r).wait_send()

            @when(j > h)
            def _():
                sum_right(j, r).wait_send()

            @when(j < h)
            def _():
                sum_left(j, r).wait_send()

        return carry

    lax.fori_loop(0, nz, drain, 0)


def shards(nz, queries, encodings, key_weight, value_weight, text_length, image_offset, cotangent):
    nx, nh, ny, nc = GRID
    tokens, width = queries.shape
    _, lmax, feat = encodings.shape
    depth = key_weight.shape[0]
    assert ny * nc * depth * nx * nh == feat * nz
    dma = pltpu.SemaphoreType.DMA
    vmem = pl.BlockSpec(memory_space=pltpu.VMEM)
    smem = pl.BlockSpec(memory_space=pltpu.SMEM)
    block = pltpu.VMEM((tokens, 2 * width), BF)
    part = pltpu.VMEM((tokens // ny, 2 * width), BF)
    line = dma((nz, CHUNKS))
    scratch = [
        pltpu.VMEM((nx, nh, ny, nc, depth, 2 * width), BF),
        pltpu.VMEM((depth, 2 * width), BF),
        pltpu.VMEM((depth, 2 * width), BF),
        pltpu.VMEM((nz, lmax, feat), BF),
        pltpu.VMEM((lmax, 2 * width), BF),
        pltpu.VMEM((2, tokens, 2 * width), BF),
        block, block, block, block,
        part, part, part, part, part, part,
        pltpu.VMEM((lmax, 2 * width), F32),
        pltpu.VMEM((lmax, 2 * width), BF),
        pltpu.VMEM((nz, lmax, feat), BF),
        pltpu.VMEM((nz, lmax, feat), BF),
        pltpu.VMEM((2, lmax, feat), F32),
        dma((2, 2, nh, 4)), dma((2, 2, nh, 4)), dma((2, nh, 2, 4)), dma((2, nh, 2, 4)), dma((2, 2)), dma((2, 2, nc)),
        dma((2, nh, 4)), dma((2, nh, 4)), dma((2,)), dma((2,)),
        pltpu.SemaphoreType.REGULAR,
        line, line, line, line,
        dma((1,)), dma((1,)), dma((ny,)), dma((1,)), dma((2, 2)), dma((2, 2)), dma((1,)), dma((ny,)),
        dma((1,)), dma((1,)), dma((ny,)), dma((1,)), dma((2, 2)), dma((2, 2)), dma((1,)), dma((ny,)),
        line, line, line, line,
    ]
    return pl.pallas_call(
        functools.partial(kernel, (nx, nh, ny, nc, nz)),
        out_shape=(
            pltpu.VMEM(queries.shape, BF),
            pltpu.VMEM(queries.shape, BF),
            pltpu.VMEM(encodings.shape, BF),
        ),
        in_specs=[smem, smem] + [vmem] * 5,
        out_specs=(vmem, vmem, vmem),
        scratch_shapes=scratch,
        compiler_params=pltpu.CompilerParams(
            collective_id=0, has_side_effects=True, vmem_limit_bytes=56 * 2**20
        ),
        name="flow_block",
    )(text_length, image_offset, queries, cotangent, encodings, key_weight, value_weight)


def solution(mesh):
    return jax.shard_map(
        functools.partial(shards, mesh.shape["head"]),
        mesh=mesh,
        in_specs=(
            P("seq", "head"),
            P("seq", None, "head"),
            P("seq", "head"),
            P("seq", "head"),
            P("seq"),
            P("seq"),
            P("seq", "head"),
        ),
        out_specs=(P("seq", "head"), P("seq", "head"), P("seq", None, "head")),
        check_vma=False,
    )
```

```python
import functools
import math

import jax
import jax.numpy as jnp
from jax import lax
from jax.experimental import pallas as pl
from jax.experimental.pallas import tpu as pltpu
from jax.sharding import PartitionSpec as P

HD = 128
GRID = (4, 2, 4, 2)
CHUNKS = 4
GATE = 6
BF = jnp.bfloat16
F32 = jnp.float32
MESH = pl.DeviceIdType.MESH


def dot(a, b, da, db):
    return lax.dot_general(a, b, (((da,), (db,)), ((), ())), preferred_element_type=F32)


def kernel(
    dims, len_ref, off_ref, q_ref, g_ref, enc_ref, wk_ref, wv_ref,
    out_ref, dq_ref, de_ref,
    w, mine, wmid, enc, kv, qg, qp, ro, rn, rp, ra, rm, rc, ba, bm, bc, dkv32, dkv, rr, rl, parts,
    wss, wrs, wts, wtr, wsx, wrx, wsb, wrb, wso, wro, gate,
    esr, err, esl, erl,
    ks, kr, ps, pr, cs, cr, fs, fr,
    bks, bkr, bps, bpr, bcs, bcr, bfs, bfr,
    rsr, rrr, rsl, rrl,
):
    nx, nh, ny, nc, nz = dims
    width = wk_ref.shape[1]
    heads = width // HD
    lmax = enc_ref.shape[1]
    tokens = q_ref.shape[0]
    piece = tokens // ny
    rows = lmax // CHUNKS
    s = lax.axis_index("seq")
    h = lax.axis_index("head")
    c = s % nc
    y = (s // nc) % ny
    zh = (s // (nc * ny)) % nh
    x = s // (nc * ny * nh)
    last = nx * nh * ny * nc - 1

    def at(x_, zh_, y_, c_):
        return ((x_ * nh + zh_) * ny + y_) * nc + c_

    def along(steps):
        z = (zh * nz + h + steps + nh * nz) % (nh * nz)
        return (at(x, z // nz, y, c), z % nz), z // nz

    sib = (at(x, zh, y, 1 - c), h)
    up, zh_up = along(nz // 2)
    down, zh_down = along(-(nz // 2))
    place = ((x, nx), (y, ny))

    def beside(axis, way):
        here, size = place[axis]
        there = (here + way + size) % size
        return there, ((at(there, zh, y, c) if axis == 0 else at(x, zh, there, c)), h)

    right = (s, h + 1)
    left = (s, h - 1)
    KC, VC = slice(0, width), slice(width, 2 * width)

    has_next = s < last
    has_prev = s > 0
    far_next = jnp.logical_and(c == nc - 1, y == ny - 1)
    far_prev = jnp.logical_and(c == 0, y == 0)
    near_next = jnp.logical_and(c == nc - 1, y < ny - 1)
    near_prev = jnp.logical_and(c == 0, y > 0)
    first_core = c == 0
    second_core = c == nc - 1
    serves = jnp.logical_and(second_core, jnp.logical_or(zh == 1, x < nx - 1))
    served = (at(jnp.where(zh == 1, x, x + 1), zh, 0, 0), h)
    goes = jnp.logical_and(second_core, jnp.logical_not(jnp.logical_and(zh == 1, x == nx - 1)))
    source = (at(x, zh, ny - 1, nc - 1), h)
    source_x = jnp.where(zh == 1, x, x - 1)

    def when(*conds):
        return pl.when(functools.reduce(jnp.logical_and, conds))

    def copy(src, dst, ss, rs, dev):
        return pltpu.make_async_remote_copy(
            src_ref=src, dst_ref=dst, send_sem=ss, recv_sem=rs, device_id=dev, device_id_type=MESH
        )

    barrier = pltpu.get_barrier_semaphore()

    def hello(dev):
        pl.semaphore_signal(barrier, inc=1, device_id=dev, device_id_type=MESH)

    hello(sib)
    for dev in (up, down):
        hello(dev)
        hello((dev[0] + 1 - 2 * c, dev[1]))

    @when(h < nz - 1)
    def _():
        hello(right)

    @when(h > 0)
    def _():
        hello(left)

    @when(near_next)
    def _():
        hello((s + 1, h))

    @when(near_prev)
    def _():
        hello((s - 1, h))

    for axis in (0, 1):
        for way in (1, -1):
            hello(beside(axis, way)[1])

    beside_source = jnp.logical_and(goes, y < ny - 1)
    far_target = jnp.logical_and(far_prev, has_prev)
    far_source = jnp.logical_and(far_next, has_next)

    @when(serves)
    def _():
        hello(served)

    @when(beside_source)
    def _():
        hello(source)

    @when(far_target)
    def _():
        for i in range(ny):
            hello((at(source_x, zh, i, nc - 1), h))

    @when(far_source)
    def _():
        for i in range(ny - 1):
            hello((at(x, zh, i, nc - 1), h))

    mine[:, KC] = wk_ref[...]
    mine[:, VC] = wv_ref[...]

    @when(first_core)
    def _():
        w[x, zh, y, 0, :, KC] = wk_ref[...]

    @when(second_core)
    def _():
        w[x, zh, y, nc - 1, :, VC] = wv_ref[...]

    enc[h] = enc_ref[0]

    @when(s == 0)
    def _():
        rp[...] = jnp.zeros_like(rp)

    @when(s == last)
    def _():
        qg[0] = jnp.zeros((tokens, 2 * width), BF)

    @when(h == 0)
    def _():
        rr[...] = jnp.zeros_like(rr)

    @when(h == nz - 1)
    def _():
        rl[...] = jnp.zeros_like(rl)

    @when(second_core, jnp.logical_not(serves))
    def _():
        ba[...] = jnp.zeros_like(ba)

    @when(second_core, jnp.logical_not(goes))
    def _():
        ra[...] = jnp.zeros_like(ra)

    def n(flag):
        return flag.astype(jnp.int32)

    count = 9 + n(h < nz - 1) + n(h > 0) + n(near_next) + n(near_prev) + n(serves) + n(beside_source)
    count = count + ny * n(far_target) + (ny - 1) * n(far_source)
    pl.semaphore_wait(barrier, count)

    def lend(i):
        cols = KC if i == 0 else VC
        return copy(mine.at[:, cols], w.at[x, zh, y, 1 - i, :, cols], wso.at[i], wro.at[i], sib)

    def cross(i, leg):
        cols, dev, z_ = (KC, up, zh_down) if i == 0 else (VC, down, zh_up)
        if leg == 0:
            return copy(mine.at[:, cols], wmid.at[:, cols], wsx.at[i, 0], wrx.at[i, 0, 0], dev)
        return copy(wmid.at[:, cols], w.at[x, z_, y, c, :, cols], wsx.at[i, 1], wrx.at[i, 1, c], (dev[0] - c + i, dev[1]))

    def cross_mid():
        for i in (0, 1):
            cross(i, 0).wait_recv()
            cross(i, 1).start()

    def cross_arrived(i):
        cols = KC if i == 0 else VC
        for core in range(nc):
            ref = w.at[x, 1 - zh, y, core, :, cols]
            copy(wmid.at[:, cols], ref, wsx.at[i, 1], wrx.at[i, 1, core], sib).wait_recv()

    def block_of(which, stage, z_, index, e, core):
        cols = KC if which == 0 else VC
        along_x = which == stage
        across = e if stage == 0 or isinstance(e, slice) else (place[which][0] + e) % place[which][1]
        if stage == 0:
            return w.at[index, z_, y, core, :, cols] if along_x else w.at[x, z_, index, core, :, cols]
        return w.at[index, z_, across, core, :, cols] if along_x else w.at[across, z_, index, core, :, cols]

    whole = slice(None)

    def hop(stage, which, z_, k):
        axis = which if stage == 0 else 1 - which
        index = place[axis][0] if k < 2 else beside(axis, -1 if k == 2 else 1)[0]
        dev = beside(axis, 1 if k % 2 == 0 else -1)[1]
        ref = block_of(which, stage, z_, index, whole, whole if k < 2 else k - 2)
        return copy(ref, ref, wss.at[stage, which, z_, k], wrs.at[stage, which, z_, k], dev)

    def second(which, z_, k, e):
        axis = 1 - which
        ref = block_of(which, 1, z_, place[axis][0], e, whole)
        dev = beside(axis, 1 if k == 0 else -1)[1]
        return copy(ref, ref, wts.at[which, z_, k, e], wtr.at[which, z_, k, e], dev)

    def seconds(which, z_, es, act):
        for e in es:
            for k in (0, 1):
                act(second(which, z_, k, e))

    def share(which, z_, d):
        here, size = place[1 - which]
        index = (here + d) % size
        ref = w.at[:, z_, index, :, :, KC] if which == 0 else w.at[index, z_, :, :, :, VC]
        return copy(ref, ref, wsb.at[which, z_, d], wrb.at[which, z_, d], sib)

    def start(cp):
        cp.start()

    def arrived(cp):
        cp.wait_recv()

    def gone(cp):
        cp.wait_send()

    def firsts(which, z_, ks_, act):
        for k in ks_:
            act(hop(0, which, z_, k))

    def lasts(which, z_, act):
        for k in (2, 3):
            act(hop(1, which, z_, k))

    def shares(which, z_, ds, act):
        for d in ds:
            act(share(which, z_, d))

    other = 1 - zh

    def spread(which):
        def one(z_):
            firsts(which, z_, (0, 1), start)
            seconds(which, z_, (0,), start)

        def two(z_):
            firsts(which, z_, (0, 1), arrived)
            firsts(which, z_, (2, 3), start)
            seconds(which, z_, (1, 3), start)

        def three(z_):
            firsts(which, z_, (2, 3), arrived)
            seconds(which, z_, (2,), start)

        def four(z_):
            seconds(which, z_, range(4), arrived)
            lasts(which, z_, start)
            shares(which, z_, (0, 1, 3), start)

        def five(z_):
            lasts(which, z_, arrived)
            shares(which, z_, (2,), start)

        near = [functools.partial(f, zh) for f in (one, two, three, four, five)]
        near[0] = lambda: (lend(which).wait_recv(), one(zh))
        far = [functools.partial(f, other) for f in (one, two, three, four, five)]
        far[0] = lambda: (cross_arrived(which), one(other))
        return near, far

    def crossing(src, mid, dst, ss, rs, i, leg):
        cols, dev = (KC, up) if i == 0 else (VC, down)
        a, b = (src, mid) if leg == 0 else (mid, dst)
        return copy(a.at[:, cols], b.at[:, cols], ss.at[i, leg], rs.at[i, leg], dev)

    def back_crossing(i, leg):
        return crossing(ba, bm, bc, bcs, bcr, i, leg)

    def there_crossing(i, leg):
        return crossing(ra, rm, rc, cs, cr, i, leg)

    def back_direct():
        return copy(qp, qg.at[0], bks.at[0], bkr.at[0], (s - 1, h))

    def back_part(i):
        return copy(qp.at[pl.ds(i * piece, piece)], ba, bps.at[i], bpr.at[0], (at(source_x, zh, i, nc - 1), h))

    def back_final(i):
        return copy(bc, qg.at[0, pl.ds(i * piece, piece)], bfs.at[0], bfr.at[i], source)

    def back_start():
        own = lax.broadcasted_iota(jnp.int32, (tokens, width), 0) >= off_ref[0]
        for cols, ref in ((KC, q_ref), (VC, g_ref)):
            block = ref[...].astype(F32)
            qg[1, :, cols] = jnp.where(own, block, 0.0).astype(BF)
            qp[:, cols] = jnp.where(own, 0.0, block).astype(BF)

        @when(has_prev, jnp.logical_not(far_prev))
        def _():
            back_direct().start()

        @when(far_target)
        def _():
            for i in range(ny):
                back_part(i).start()

    def back_one():
        @when(serves)
        def _():
            back_part(0).wait_recv()

        for i in (0, 1):
            back_crossing(i, 0).start()

    def back_two():
        for i in (0, 1):
            back_crossing(i, 0).wait_recv()
            back_crossing(i, 1).start()

    def back_three():
        for i in (0, 1):
            back_crossing(i, 1).wait_recv()
        for i in range(ny - 1):

            @when(goes, y == i)
            def _():
                back_final(i).start()

        @when(goes, y == ny - 1)
        def _():
            qg[0, (ny - 1) * piece :, :] = bc[...]

    def back_arrived():
        @when(has_next)
        def _():
            @when(jnp.logical_not(far_next))
            def _():
                back_direct().wait_recv()

            @when(far_next)
            def _():
                for i in range(ny - 1):
                    back_final(i).wait_recv()

    def send_enc_right(j, r):
        ref = enc.at[j, pl.ds(r * rows, rows)]
        return copy(ref, ref, esr.at[j, r], err.at[j, r], right)

    def send_enc_left(j, r):
        ref = enc.at[j, pl.ds(r * rows, rows)]
        return copy(ref, ref, esl.at[j, r], erl.at[j, r], left)

    def open_gate():
        pl.semaphore_signal(gate, inc=1, device_id=sib, device_id_type=MESH)

    def project(f):
        if nx * nh == nz:
            block = w[f // nh, f % nh].reshape(-1, 2 * width)
        else:
            block = w[f].reshape(-1, 2 * width)
        return dot(enc[f], block, 1, 0)

    def gather(todo, projecting):
        for st in range(nz):
            for r in range(CHUNKS):
                if st > 0:

                    @when(h - st >= 0)
                    def _():
                        send_enc_right(h - st, r).wait_recv()

                if st < nz - 1:

                    @when(h - st >= 0, h < nz - 1)
                    def _():
                        send_enc_right(h - st, r).start()

                if st > 0:

                    @when(h + st < nz)
                    def _():
                        send_enc_left(h + st, r).wait_recv()

                if st < nz - 1:

                    @when(h + st < nz, h > 0)
                    def _():
                        send_enc_left(h + st, r).start()

            for task in todo.get(st, ()):
                task()
            if projecting:
                for d in {nz - 4: (0, 1), nz - 3: (2, 3), nz - 2: (4, 5), nz - 1: (6, 7)}.get(st, ()):
                    if d == 0:
                        dkv32[...] = project(h)
                    else:

                        @when(h - d >= 0)
                        def _():
                            dkv32[...] += project(h - d)

                        @when(h + d < nz)
                        def _():
                            dkv32[...] += project(h + d)

    for i in (0, 1):
        cross(i, 0).start()

    @when(second_core)
    def _():
        lend(0).start()
        near, far = spread(1)
        gather(
            {
                0: (back_start, near[0]),
                1: (near[1], cross_mid),
                2: (near[2],),
                3: (near[3], back_one),
                4: (far[0], near[4]),
                5: (far[1],),
                GATE: (far[2], back_two, open_gate),
            },
            False,
        )
        far[3]()
        far[4]()
        back_three()
        dkv32[...] = jnp.zeros_like(dkv32)
        if nx * nh == nz:
            groups = ((zh, nh), (other, nh))
        else:
            groups = (None, (0, 1))
        for z_, group in zip((zh, other), groups):
            shares(0, z_, range(4), arrived)
            if group is not None:

                def two(f, carry):
                    first, step = group
                    dkv32[...] += project(first + 2 * f * step) + project(first + (2 * f + 1) * step)
                    return carry

                lax.fori_loop(0, nz // (2 * group[1]), two, 0)

    @when(first_core)
    def _():
        lend(1).start()
        near, far = spread(0)
        for task in (
            near[0], back_start, near[1], cross_mid, near[2], near[3], far[0], near[4], far[1], far[2],
        ):
            task()
        pl.semaphore_wait(gate, 1)

        def whole_weights():
            for z_ in (0, 1):
                shares(1, z_, range(4), arrived)

        gather({0: (far[3],), 1: (far[4],), 3: (whole_weights,)}, True)

    kv[...] = dkv32[...].astype(BF)

    scale = 1.0 / math.sqrt(HD)
    ok = lax.broadcasted_iota(jnp.int32, (1, lmax), 1) < len_ref[0]
    for b in (1, 0):
        if b == 0:
            back_arrived()
        result = ro if b == 1 else rn
        for a in range(heads):
            kc = slice(a * HD, (a + 1) * HD)
            vc = slice(width + a * HD, width + (a + 1) * HD)
            q = qg[b, :, kc]
            g = qg[b, :, vc]
            k = kv[:, kc]
            v = kv[:, vc]
            scores = jnp.where(ok, dot(q, k, 1, 1), -1e30)
            expo = jnp.exp2((scores - jnp.max(scores, axis=-1, keepdims=True)) * (scale * math.log2(math.e)))
            inverse = 1.0 / jnp.sum(expo, axis=-1, keepdims=True)
            probs = expo * inverse
            dprobs = dot(g, v, 1, 1)
            delta = jnp.sum(probs * dprobs, axis=-1, keepdims=True)
            ds = ((expo * (inverse * scale)) * (dprobs - delta)).astype(BF)
            pb = probs.astype(BF)
            result[:, kc] = dot(pb, v, 1, 0).astype(BF)
            result[:, vc] = dot(ds, k, 1, 0).astype(BF)
            dk = dot(ds, q, 0, 0)
            dv = dot(pb, g, 0, 0)
            if b == 1:
                dkv32[:, kc] = dk
                dkv32[:, vc] = dv
            else:
                dkv[:, kc] = (dkv32[:, kc] + dk).astype(BF)
                dkv[:, vc] = (dkv32[:, vc] + dv).astype(BF)

    def there_direct():
        return copy(rn, rp, ks.at[0], kr.at[0], (s + 1, h))

    def there_part(i):
        return copy(rn.at[pl.ds(i * piece, piece)], ra, ps.at[i], pr.at[0], (at(x, zh, i, nc - 1), h))

    def there_final(i):
        return copy(rc, rp.at[pl.ds(i * piece, piece)], fs.at[0], fr.at[i], served)

    def there_one():
        @when(goes, y < ny - 1)
        def _():
            there_part(0).wait_recv()

        for i in (0, 1):
            there_crossing(i, 0).start()

    def there_two():
        for i in (0, 1):
            there_crossing(i, 0).wait_recv()
            there_crossing(i, 1).start()

    def there_three():
        for i in (0, 1):
            there_crossing(i, 1).wait_recv()
        for i in range(ny):

            @when(serves, y == i)
            def _():
                there_final(i).start()

    @when(has_next, jnp.logical_not(far_next))
    def _():
        there_direct().start()

    @when(far_source)
    def _():
        for i in range(ny - 1):
            there_part(i).start()
        ra[...] = rn[(ny - 1) * piece :, :]

    def sum_right(j, r):
        ref = rr.at[j, pl.ds(r * rows, rows)]
        return copy(ref, ref, rsr.at[j, r], rrr.at[j, r], right)

    def sum_left(j, r):
        ref = rl.at[j, pl.ds(r * rows, rows)]
        return copy(ref, ref, rsl.at[j, r], rrl.at[j, r], left)

    def partial(j):
        if nx * nh == nz:
            block = w[j // nh, j % nh].reshape(-1, 2 * width)
        else:
            block = w[j].reshape(-1, 2 * width)
        return dot(dkv[...], block, 1, 1)

    def reduce_step(t, carry):
        going_right = jnp.logical_and(t >= h, h < nz - 1)
        going_left = jnp.logical_and(t >= nz - 1 - h, h > 0)
        jr = nz - 1 + h - t
        jl = t - (nz - 1 - h)

        @when(going_right)
        def _():
            parts[0] = partial(jr)

        @when(going_left)
        def _():
            parts[1] = partial(jl)

        for r in range(CHUNKS):
            here = pl.ds(r * rows, rows)

            @when(going_right)
            def _():
                @when(h > 0)
                def _():
                    sum_right(jr, r).wait_recv()

                rr[jr, here, :] = (parts[0, here, :] + rr[jr, here, :].astype(F32)).astype(BF)
                sum_right(jr, r).start()

            @when(going_left)
            def _():
                @when(h < nz - 1)
                def _():
                    sum_left(jl, r).wait_recv()

                rl[jl, here, :] = (parts[1, here, :] + rl[jl, here, :].astype(F32)).astype(BF)
                sum_left(jl, r).start()

        @when(second_core, t == 1)
        def _():
            there_one()

        @when(second_core, t == 3)
        def _():
            there_two()

        @when(second_core, t == 5)
        def _():
            there_three()

        return carry

    lax.fori_loop(0, nz - 1, reduce_step, 0)

    parts[0] = partial(h)
    for r in range(CHUNKS):
        here = pl.ds(r * rows, rows)

        @when(h > 0)
        def _():
            sum_right(h, r).wait_recv()

        @when(h < nz - 1)
        def _():
            sum_left(h, r).wait_recv()

        total = parts[0, here, :] + rr[h, here, :].astype(F32) + rl[h, here, :].astype(F32)
        de_ref[0, here, :] = total.astype(BF)

    @when(has_prev)
    def _():
        @when(jnp.logical_not(far_prev))
        def _():
            there_direct().wait_recv()

        @when(far_prev)
        def _():
            for i in range(ny):
                there_final(i).wait_recv()

    own = lax.broadcasted_iota(jnp.int32, (tokens, width), 0) >= off_ref[0]
    for cols, ref in ((KC, out_ref), (VC, dq_ref)):
        ref[...] = jnp.where(own, ro[:, cols].astype(F32), rp[:, cols].astype(F32)).astype(BF)

    for i in (0, 1):
        for leg in (0, 1):
            cross(i, leg).wait_send()

    def weights_gone(which):
        lend(1 - which).wait_send()
        for z_ in (0, 1):
            shares(which, z_, range(4), gone)
            firsts(which, z_, range(4), gone)
            seconds(which, z_, range(4), gone)
            lasts(which, z_, gone)

    @when(first_core)
    def _():
        weights_gone(0)

    @when(second_core)
    def _():
        weights_gone(1)
        for i in (0, 1):
            for leg in (0, 1):
                back_crossing(i, leg).wait_send()
                there_crossing(i, leg).wait_send()

        @when(goes, y < ny - 1)
        def _():
            back_final(0).wait_send()

        @when(serves)
        def _():
            there_final(0).wait_send()

    @when(has_prev, jnp.logical_not(far_prev))
    def _():
        back_direct().wait_send()

    @when(far_target)
    def _():
        for i in range(ny):
            back_part(i).wait_send()

    @when(has_next, jnp.logical_not(far_next))
    def _():
        there_direct().wait_send()

    @when(far_source)
    def _():
        for i in range(ny - 1):
            there_part(i).wait_send()

    def drain(j, carry):
        for r in range(CHUNKS):

            @when(j <= h, h < nz - 1)
            def _():
                send_enc_right(j, r).wait_send()

            @when(j >= h, h > 0)
            def _():
                send_enc_left(j, r).wait_send()

            @when(j > h)
            def _():
                sum_right(j, r).wait_send()

            @when(j < h)
            def _():
                sum_left(j, r).wait_send()

        return carry

    lax.fori_loop(0, nz, drain, 0)


def shards(nz, queries, encodings, key_weight, value_weight, text_length, image_offset, cotangent):
    nx, nh, ny, nc = GRID
    tokens, width = queries.shape
    _, lmax, feat = encodings.shape
    depth = key_weight.shape[0]
    assert ny * nc * depth * nx * nh == feat * nz
    dma = pltpu.SemaphoreType.DMA
    vmem = pl.BlockSpec(memory_space=pltpu.VMEM)
    smem = pl.BlockSpec(memory_space=pltpu.SMEM)
    block = pltpu.VMEM((tokens, 2 * width), BF)
    part = pltpu.VMEM((tokens // ny, 2 * width), BF)
    line = dma((nz, CHUNKS))
    scratch = [
        pltpu.VMEM((nx, nh, ny, nc, depth, 2 * width), BF),
        pltpu.VMEM((depth, 2 * width), BF),
        pltpu.VMEM((depth, 2 * width), BF),
        pltpu.VMEM((nz, lmax, feat), BF),
        pltpu.VMEM((lmax, 2 * width), BF),
        pltpu.VMEM((2, tokens, 2 * width), BF),
        block, block, block, block,
        part, part, part, part, part, part,
        pltpu.VMEM((lmax, 2 * width), F32),
        pltpu.VMEM((lmax, 2 * width), BF),
        pltpu.VMEM((nz, lmax, feat), BF),
        pltpu.VMEM((nz, lmax, feat), BF),
        pltpu.VMEM((2, lmax, feat), F32),
        dma((2, 2, nh, 4)), dma((2, 2, nh, 4)), dma((2, nh, 2, 4)), dma((2, nh, 2, 4)), dma((2, 2)), dma((2, 2, nc)),
        dma((2, nh, 4)), dma((2, nh, 4)), dma((2,)), dma((2,)),
        pltpu.SemaphoreType.REGULAR,
        line, line, line, line,
        dma((1,)), dma((1,)), dma((ny,)), dma((1,)), dma((2, 2)), dma((2, 2)), dma((1,)), dma((ny,)),
        dma((1,)), dma((1,)), dma((ny,)), dma((1,)), dma((2, 2)), dma((2, 2)), dma((1,)), dma((ny,)),
        line, line, line, line,
    ]
    return pl.pallas_call(
        functools.partial(kernel, (nx, nh, ny, nc, nz)),
        out_shape=(
            pltpu.VMEM(queries.shape, BF),
            pltpu.VMEM(queries.shape, BF),
            pltpu.VMEM(encodings.shape, BF),
        ),
        in_specs=[smem, smem] + [vmem] * 5,
        out_specs=(vmem, vmem, vmem),
        scratch_shapes=scratch,
        compiler_params=pltpu.CompilerParams(
            collective_id=0, has_side_effects=True, vmem_limit_bytes=56 * 2**20
        ),
        name="flow_block",
    )(text_length, image_offset, queries, cotangent, encodings, key_weight, value_weight)


def solution(mesh):
    return jax.shard_map(
        functools.partial(shards, mesh.shape["head"]),
        mesh=mesh,
        in_specs=(
            P("seq", "head"),
            P("seq", None, "head"),
            P("seq", "head"),
            P("seq", "head"),
            P("seq"),
            P("seq"),
            P("seq", "head"),
        ),
        out_specs=(P("seq", "head"), P("seq", "head"), P("seq", None, "head")),
        check_vma=False,
    )
```

```python
import functools
import math

import jax
import jax.numpy as jnp
from jax import lax
from jax.experimental import pallas as pl
from jax.experimental.pallas import tpu as pltpu
from jax.sharding import PartitionSpec as P

HD = 128
GRID = (4, 2, 4, 2)
CHUNKS = 4
GATE = 6
BF = jnp.bfloat16
F32 = jnp.float32
MESH = pl.DeviceIdType.MESH


def dot(a, b, da, db):
    return lax.dot_general(a, b, (((da,), (db,)), ((), ())), preferred_element_type=F32)


def kernel(
    dims, len_ref, off_ref, q_ref, g_ref, enc_ref, wk_ref, wv_ref,
    out_ref, dq_ref, de_ref,
    w, mine, wmid, enc, kv, qg, qp, ro, rn, rp, ra, rm, rc, ba, bm, bc, dkv32, dkv, rr, rl, parts,
    wss, wrs, wts, wtr, wsx, wrx, wsb, wrb, wso, wro, gate,
    esr, err, esl, erl,
    ks, kr, ps, pr, cs, cr, fs, fr,
    bks, bkr, bps, bpr, bcs, bcr, bfs, bfr,
    rsr, rrr, rsl, rrl,
):
    nx, nh, ny, nc, nz = dims
    width = wk_ref.shape[1]
    heads = width // HD
    lmax = enc_ref.shape[1]
    tokens = q_ref.shape[0]
    piece = tokens // ny
    rows = lmax // CHUNKS
    s = lax.axis_index("seq")
    h = lax.axis_index("head")
    c = s % nc
    y = (s // nc) % ny
    zh = (s // (nc * ny)) % nh
    x = s // (nc * ny * nh)
    last = nx * nh * ny * nc - 1

    def at(x_, zh_, y_, c_):
        return ((x_ * nh + zh_) * ny + y_) * nc + c_

    def along(steps):
        z = (zh * nz + h + steps + nh * nz) % (nh * nz)
        return (at(x, z // nz, y, c), z % nz), z // nz

    sib = (at(x, zh, y, 1 - c), h)
    up, zh_up = along(nz // 2)
    down, zh_down = along(-(nz // 2))
    place = ((x, nx), (y, ny))

    def beside(axis, way):
        here, size = place[axis]
        there = (here + way + size) % size
        return there, ((at(there, zh, y, c) if axis == 0 else at(x, zh, there, c)), h)

    right = (s, h + 1)
    left = (s, h - 1)
    KC, VC = slice(0, width), slice(width, 2 * width)

    has_next = s < last
    has_prev = s > 0
    far_next = jnp.logical_and(c == nc - 1, y == ny - 1)
    far_prev = jnp.logical_and(c == 0, y == 0)
    near_next = jnp.logical_and(c == nc - 1, y < ny - 1)
    near_prev = jnp.logical_and(c == 0, y > 0)
    first_core = c == 0
    second_core = c == nc - 1
    serves = jnp.logical_and(second_core, jnp.logical_or(zh == 1, x < nx - 1))
    served = (at(jnp.where(zh == 1, x, x + 1), zh, 0, 0), h)
    goes = jnp.logical_and(second_core, jnp.logical_not(jnp.logical_and(zh == 1, x == nx - 1)))
    source = (at(x, zh, ny - 1, nc - 1), h)
    source_x = jnp.where(zh == 1, x, x - 1)

    def when(*conds):
        return pl.when(functools.reduce(jnp.logical_and, conds))

    def copy(src, dst, ss, rs, dev):
        return pltpu.make_async_remote_copy(
            src_ref=src, dst_ref=dst, send_sem=ss, recv_sem=rs, device_id=dev, device_id_type=MESH
        )

    barrier = pltpu.get_barrier_semaphore()

    def hello(dev):
        pl.semaphore_signal(barrier, inc=1, device_id=dev, device_id_type=MESH)

    hello(sib)
    for dev in (up, down):
        hello(dev)
        hello((dev[0] + 1 - 2 * c, dev[1]))

    @when(h < nz - 1)
    def _():
        hello(right)

    @when(h > 0)
    def _():
        hello(left)

    @when(near_next)
    def _():
        hello((s + 1, h))

    @when(near_prev)
    def _():
        hello((s - 1, h))

    for axis in (0, 1):
        for way in (1, -1):
            hello(beside(axis, way)[1])

    beside_source = jnp.logical_and(goes, y < ny - 1)
    far_target = jnp.logical_and(far_prev, has_prev)
    far_source = jnp.logical_and(far_next, has_next)

    @when(serves)
    def _():
        hello(served)

    @when(beside_source)
    def _():
        hello(source)

    @when(far_target)
    def _():
        for i in range(ny):
            hello((at(source_x, zh, i, nc - 1), h))

    @when(far_source)
    def _():
        for i in range(ny - 1):
            hello((at(x, zh, i, nc - 1), h))

    mine[:, KC] = wk_ref[...]
    mine[:, VC] = wv_ref[...]

    @when(first_core)
    def _():
        w[x, zh, y, 0, :, KC] = wk_ref[...]

    @when(second_core)
    def _():
        w[x, zh, y, nc - 1, :, VC] = wv_ref[...]

    enc[h] = enc_ref[0]

    @when(s == 0)
    def _():
        rp[...] = jnp.zeros_like(rp)

    @when(s == last)
    def _():
        qg[0] = jnp.zeros((tokens, 2 * width), BF)

    @when(h == 0)
    def _():
        rr[...] = jnp.zeros_like(rr)

    @when(h == nz - 1)
    def _():
        rl[...] = jnp.zeros_like(rl)

    @when(second_core, jnp.logical_not(serves))
    def _():
        ba[...] = jnp.zeros_like(ba)

    @when(second_core, jnp.logical_not(goes))
    def _():
        ra[...] = jnp.zeros_like(ra)

    def n(flag):
        return flag.astype(jnp.int32)

    count = 9 + n(h < nz - 1) + n(h > 0) + n(near_next) + n(near_prev) + n(serves) + n(beside_source)
    count = count + ny * n(far_target) + (ny - 1) * n(far_source)
    pl.semaphore_wait(barrier, count)

    def lend(i):
        cols = KC if i == 0 else VC
        return copy(mine.at[:, cols], w.at[x, zh, y, 1 - i, :, cols], wso.at[i], wro.at[i], sib)

    def cross(i, leg):
        cols, dev, z_ = (KC, up, zh_down) if i == 0 else (VC, down, zh_up)
        if leg == 0:
            return copy(mine.at[:, cols], wmid.at[:, cols], wsx.at[i, 0], wrx.at[i, 0, 0], dev)
        return copy(wmid.at[:, cols], w.at[x, z_, y, c, :, cols], wsx.at[i, 1], wrx.at[i, 1, c], (dev[0] - c + i, dev[1]))

    def cross_mid():
        for i in (0, 1):
            cross(i, 0).wait_recv()
            cross(i, 1).start()

    def cross_arrived(i):
        cols = KC if i == 0 else VC
        for core in range(nc):
            ref = w.at[x, 1 - zh, y, core, :, cols]
            copy(wmid.at[:, cols], ref, wsx.at[i, 1], wrx.at[i, 1, core], sib).wait_recv()

    def block_of(which, stage, z_, index, e, core):
        cols = KC if which == 0 else VC
        along_x = which == stage
        across = e if stage == 0 or isinstance(e, slice) else (place[which][0] + e) % place[which][1]
        if stage == 0:
            return w.at[index, z_, y, core, :, cols] if along_x else w.at[x, z_, index, core, :, cols]
        return w.at[index, z_, across, core, :, cols] if along_x else w.at[across, z_, index, core, :, cols]

    whole = slice(None)

    def hop(stage, which, z_, k):
        axis = which if stage == 0 else 1 - which
        index = place[axis][0] if k < 2 else beside(axis, -1 if k == 2 else 1)[0]
        dev = beside(axis, 1 if k % 2 == 0 else -1)[1]
        ref = block_of(which, stage, z_, index, whole, whole if k < 2 else k - 2)
        return copy(ref, ref, wss.at[stage, which, z_, k], wrs.at[stage, which, z_, k], dev)

    def second(which, z_, k, e):
        axis = 1 - which
        ref = block_of(which, 1, z_, place[axis][0], e, whole)
        dev = beside(axis, 1 if k == 0 else -1)[1]
        return copy(ref, ref, wts.at[which, z_, k, e], wtr.at[which, z_, k, e], dev)

    def seconds(which, z_, es, act):
        for e in es:
            for k in (0, 1):
                act(second(which, z_, k, e))

    def share(which, z_, d):
        here, size = place[1 - which]
        index = (here + d) % size
        ref = w.at[:, z_, index, :, :, KC] if which == 0 else w.at[index, z_, :, :, :, VC]
        return copy(ref, ref, wsb.at[which, z_, d], wrb.at[which, z_, d], sib)

    def start(cp):
        cp.start()

    def arrived(cp):
        cp.wait_recv()

    def gone(cp):
        cp.wait_send()

    def firsts(which, z_, ks_, act):
        for k in ks_:
            act(hop(0, which, z_, k))

    def lasts(which, z_, act):
        for k in (2, 3):
            act(hop(1, which, z_, k))

    def shares(which, z_, ds, act):
        for d in ds:
            act(share(which, z_, d))

    other = 1 - zh

    def spread(which):
        def one(z_):
            firsts(which, z_, (0, 1), start)
            seconds(which, z_, (0,), start)

        def two(z_):
            firsts(which, z_, (0, 1), arrived)
            firsts(which, z_, (2, 3), start)
            seconds(which, z_, (1, 3), start)

        def three(z_):
            firsts(which, z_, (2, 3), arrived)
            seconds(which, z_, (2,), start)

        def four(z_):
            seconds(which, z_, range(4), arrived)
            lasts(which, z_, start)
            shares(which, z_, (0, 1, 3), start)

        def five(z_):
            lasts(which, z_, arrived)
            shares(which, z_, (2,), start)

        near = [functools.partial(f, zh) for f in (one, two, three, four, five)]
        near[0] = lambda: (lend(which).wait_recv(), one(zh))
        far = [functools.partial(f, other) for f in (one, two, three, four, five)]
        far[0] = lambda: (cross_arrived(which), one(other))
        return near, far

    def crossing(src, mid, dst, ss, rs, i, leg):
        cols, dev = (KC, up) if i == 0 else (VC, down)
        a, b = (src, mid) if leg == 0 else (mid, dst)
        return copy(a.at[:, cols], b.at[:, cols], ss.at[i, leg], rs.at[i, leg], dev)

    def back_crossing(i, leg):
        return crossing(ba, bm, bc, bcs, bcr, i, leg)

    def there_crossing(i, leg):
        return crossing(ra, rm, rc, cs, cr, i, leg)

    def back_direct():
        return copy(qp, qg.at[0], bks.at[0], bkr.at[0], (s - 1, h))

    def back_part(i):
        return copy(qp.at[pl.ds(i * piece, piece)], ba, bps.at[i], bpr.at[0], (at(source_x, zh, i, nc - 1), h))

    def back_final(i):
        return copy(bc, qg.at[0, pl.ds(i * piece, piece)], bfs.at[0], bfr.at[i], source)

    def back_start():
        own = lax.broadcasted_iota(jnp.int32, (tokens, width), 0) >= off_ref[0]
        for cols, ref in ((KC, q_ref), (VC, g_ref)):
            block = ref[...].astype(F32)
            qg[1, :, cols] = jnp.where(own, block, 0.0).astype(BF)
            qp[:, cols] = jnp.where(own, 0.0, block).astype(BF)

        @when(has_prev, jnp.logical_not(far_prev))
        def _():
            back_direct().start()

        @when(far_target)
        def _():
            for i in range(ny):
                back_part(i).start()

    def back_one():
        @when(serves)
        def _():
            back_part(0).wait_recv()

        for i in (0, 1):
            back_crossing(i, 0).start()

    def back_two():
        for i in (0, 1):
            back_crossing(i, 0).wait_recv()
            back_crossing(i, 1).start()

    def back_three():
        for i in (0, 1):
            back_crossing(i, 1).wait_recv()
        for i in range(ny - 1):

            @when(goes, y == i)
            def _():
                back_final(i).start()

        @when(goes, y == ny - 1)
        def _():
            qg[0, (ny - 1) * piece :, :] = bc[...]

    def back_arrived():
        @when(has_next)
        def _():
            @when(jnp.logical_not(far_next))
            def _():
                back_direct().wait_recv()

            @when(far_next)
            def _():
                for i in range(ny - 1):
                    back_final(i).wait_recv()

    def send_enc_right(j, r):
        ref = enc.at[j, pl.ds(r * rows, rows)]
        return copy(ref, ref, esr.at[j, r], err.at[j, r], right)

    def send_enc_left(j, r):
        ref = enc.at[j, pl.ds(r * rows, rows)]
        return copy(ref, ref, esl.at[j, r], erl.at[j, r], left)

    def open_gate():
        pl.semaphore_signal(gate, inc=1, device_id=sib, device_id_type=MESH)

    def project(f):
        if nx * nh == nz:
            block = w[f // nh, f % nh].reshape(-1, 2 * width)
        else:
            block = w[f].reshape(-1, 2 * width)
        return dot(enc[f], block, 1, 0)

    def gather(todo, projecting):
        for st in range(nz):
            for r in range(CHUNKS):
                if st > 0:

                    @when(h - st >= 0)
                    def _():
                        send_enc_right(h - st, r).wait_recv()

                if st < nz - 1:

                    @when(h - st >= 0, h < nz - 1)
                    def _():
                        send_enc_right(h - st, r).start()

                if st > 0:

                    @when(h + st < nz)
                    def _():
                        send_enc_left(h + st, r).wait_recv()

                if st < nz - 1:

                    @when(h + st < nz, h > 0)
                    def _():
                        send_enc_left(h + st, r).start()

            for task in todo.get(st, ()):
                task()
            if projecting:
                for d in {nz - 4: (0, 1), nz - 3: (2, 3), nz - 2: (4, 5), nz - 1: (6, 7)}.get(st, ()):
                    if d == 0:
                        dkv32[...] = project(h)
                    else:
                        low, high = h - d >= 0, h + d < nz

                        @when(low, high)
                        def _():
                            dkv32[...] += project(h - d) + project(h + d)

                        @when(low, jnp.logical_not(high))
                        def _():
                            dkv32[...] += project(h - d)

                        @when(high, jnp.logical_not(low))
                        def _():
                            dkv32[...] += project(h + d)

    for i in (0, 1):
        cross(i, 0).start()

    @when(second_core)
    def _():
        lend(0).start()
        near, far = spread(1)
        gather(
            {
                0: (back_start, near[0]),
                1: (near[1], cross_mid),
                2: (near[2],),
                3: (near[3], back_one),
                4: (far[0], near[4]),
                5: (far[1],),
                GATE: (far[2], back_two, open_gate),
            },
            False,
        )
        far[3]()
        far[4]()
        back_three()
        dkv32[...] = jnp.zeros_like(dkv32)
        if nx * nh == nz:
            groups = ((zh, nh), (other, nh))
        else:
            groups = (None, (0, 1))
        for z_, group in zip((zh, other), groups):
            shares(0, z_, range(4), arrived)
            if group is not None:

                def two(f, carry):
                    first, step = group
                    dkv32[...] += project(first + 2 * f * step) + project(first + (2 * f + 1) * step)
                    return carry

                lax.fori_loop(0, nz // (2 * group[1]), two, 0)

    @when(first_core)
    def _():
        lend(1).start()
        near, far = spread(0)
        for task in (
            near[0], back_start, near[1], cross_mid, near[2], near[3], far[0], near[4], far[1], far[2],
        ):
            task()
        pl.semaphore_wait(gate, 1)

        def whole_weights():
            for z_ in (0, 1):
                shares(1, z_, range(4), arrived)

        gather({0: (far[3],), 1: (far[4],), 3: (whole_weights,)}, True)

    kv[...] = dkv32[...].astype(BF)

    scale = 1.0 / math.sqrt(HD)
    ok = lax.broadcasted_iota(jnp.int32, (1, lmax), 1) < len_ref[0]
    for b in (1, 0):
        if b == 0:
            back_arrived()
        result = ro if b == 1 else rn
        for a in range(heads):
            kc = slice(a * HD, (a + 1) * HD)
            vc = slice(width + a * HD, width + (a + 1) * HD)
            q = qg[b, :, kc]
            g = qg[b, :, vc]
            k = kv[:, kc]
            v = kv[:, vc]
            scores = jnp.where(ok, dot(q, k, 1, 1), -1e30)
            expo = jnp.exp2((scores - jnp.max(scores, axis=-1, keepdims=True)) * (scale * math.log2(math.e)))
            inverse = 1.0 / jnp.sum(expo, axis=-1, keepdims=True)
            probs = expo * inverse
            dprobs = dot(g, v, 1, 1)
            delta = jnp.sum(probs * dprobs, axis=-1, keepdims=True)
            ds = ((expo * (inverse * scale)) * (dprobs - delta)).astype(BF)
            pb = probs.astype(BF)
            result[:, kc] = dot(pb, v, 1, 0).astype(BF)
            result[:, vc] = dot(ds, k, 1, 0).astype(BF)
            dk = dot(ds, q, 0, 0)
            dv = dot(pb, g, 0, 0)
            if b == 1:
                dkv32[:, kc] = dk
                dkv32[:, vc] = dv
            else:
                dkv[:, kc] = (dkv32[:, kc] + dk).astype(BF)
                dkv[:, vc] = (dkv32[:, vc] + dv).astype(BF)

    def there_direct():
        return copy(rn, rp, ks.at[0], kr.at[0], (s + 1, h))

    def there_part(i):
        return copy(rn.at[pl.ds(i * piece, piece)], ra, ps.at[i], pr.at[0], (at(x, zh, i, nc - 1), h))

    def there_final(i):
        return copy(rc, rp.at[pl.ds(i * piece, piece)], fs.at[0], fr.at[i], served)

    def there_one():
        @when(goes, y < ny - 1)
        def _():
            there_part(0).wait_recv()

        for i in (0, 1):
            there_crossing(i, 0).start()

    def there_two():
        for i in (0, 1):
            there_crossing(i, 0).wait_recv()
            there_crossing(i, 1).start()

    def there_three():
        for i in (0, 1):
            there_crossing(i, 1).wait_recv()
        for i in range(ny):

            @when(serves, y == i)
            def _():
                there_final(i).start()

    @when(has_next, jnp.logical_not(far_next))
    def _():
        there_direct().start()

    @when(far_source)
    def _():
        for i in range(ny - 1):
            there_part(i).start()
        ra[...] = rn[(ny - 1) * piece :, :]

    def sum_right(j, r):
        ref = rr.at[j, pl.ds(r * rows, rows)]
        return copy(ref, ref, rsr.at[j, r], rrr.at[j, r], right)

    def sum_left(j, r):
        ref = rl.at[j, pl.ds(r * rows, rows)]
        return copy(ref, ref, rsl.at[j, r], rrl.at[j, r], left)

    def partial(j):
        if nx * nh == nz:
            block = w[j // nh, j % nh].reshape(-1, 2 * width)
        else:
            block = w[j].reshape(-1, 2 * width)
        return dot(dkv[...], block, 1, 1)

    def reduce_step(t, carry):
        going_right = jnp.logical_and(t >= h, h < nz - 1)
        going_left = jnp.logical_and(t >= nz - 1 - h, h > 0)
        jr = nz - 1 + h - t
        jl = t - (nz - 1 - h)

        @when(going_right)
        def _():
            parts[0] = partial(jr)

        @when(going_left)
        def _():
            parts[1] = partial(jl)

        for r in range(CHUNKS):
            here = pl.ds(r * rows, rows)

            @when(going_right)
            def _():
                @when(h > 0)
                def _():
                    sum_right(jr, r).wait_recv()

                rr[jr, here, :] = (parts[0, here, :] + rr[jr, here, :].astype(F32)).astype(BF)
                sum_right(jr, r).start()

            @when(going_left)
            def _():
                @when(h < nz - 1)
                def _():
                    sum_left(jl, r).wait_recv()

                rl[jl, here, :] = (parts[1, here, :] + rl[jl, here, :].astype(F32)).astype(BF)
                sum_left(jl, r).start()

        @when(second_core, t == 1)
        def _():
            there_one()

        @when(second_core, t == 3)
        def _():
            there_two()

        @when(second_core, t == 5)
        def _():
            there_three()

        return carry

    lax.fori_loop(0, nz - 1, reduce_step, 0)

    parts[0] = partial(h)
    for r in range(CHUNKS):
        here = pl.ds(r * rows, rows)

        @when(h > 0)
        def _():
            sum_right(h, r).wait_recv()

        @when(h < nz - 1)
        def _():
            sum_left(h, r).wait_recv()

        total = parts[0, here, :] + rr[h, here, :].astype(F32) + rl[h, here, :].astype(F32)
        de_ref[0, here, :] = total.astype(BF)

    @when(has_prev)
    def _():
        @when(jnp.logical_not(far_prev))
        def _():
            there_direct().wait_recv()

        @when(far_prev)
        def _():
            for i in range(ny):
                there_final(i).wait_recv()

    own = lax.broadcasted_iota(jnp.int32, (tokens, width), 0) >= off_ref[0]
    for cols, ref in ((KC, out_ref), (VC, dq_ref)):
        ref[...] = jnp.where(own, ro[:, cols].astype(F32), rp[:, cols].astype(F32)).astype(BF)

    for i in (0, 1):
        for leg in (0, 1):
            cross(i, leg).wait_send()

    def weights_gone(which):
        lend(1 - which).wait_send()
        for z_ in (0, 1):
            shares(which, z_, range(4), gone)
            firsts(which, z_, range(4), gone)
            seconds(which, z_, range(4), gone)
            lasts(which, z_, gone)

    @when(first_core)
    def _():
        weights_gone(0)

    @when(second_core)
    def _():
        weights_gone(1)
        for i in (0, 1):
            for leg in (0, 1):
                back_crossing(i, leg).wait_send()
                there_crossing(i, leg).wait_send()

        @when(goes, y < ny - 1)
        def _():
            back_final(0).wait_send()

        @when(serves)
        def _():
            there_final(0).wait_send()

    @when(has_prev, jnp.logical_not(far_prev))
    def _():
        back_direct().wait_send()

    @when(far_target)
    def _():
        for i in range(ny):
            back_part(i).wait_send()

    @when(has_next, jnp.logical_not(far_next))
    def _():
        there_direct().wait_send()

    @when(far_source)
    def _():
        for i in range(ny - 1):
            there_part(i).wait_send()

    def drain(j, carry):
        for r in range(CHUNKS):

            @when(j <= h, h < nz - 1)
            def _():
                send_enc_right(j, r).wait_send()

            @when(j >= h, h > 0)
            def _():
                send_enc_left(j, r).wait_send()

            @when(j > h)
            def _():
                sum_right(j, r).wait_send()

            @when(j < h)
            def _():
                sum_left(j, r).wait_send()

        return carry

    lax.fori_loop(0, nz, drain, 0)


def shards(nz, queries, encodings, key_weight, value_weight, text_length, image_offset, cotangent):
    nx, nh, ny, nc = GRID
    tokens, width = queries.shape
    _, lmax, feat = encodings.shape
    depth = key_weight.shape[0]
    assert ny * nc * depth * nx * nh == feat * nz
    dma = pltpu.SemaphoreType.DMA
    vmem = pl.BlockSpec(memory_space=pltpu.VMEM)
    smem = pl.BlockSpec(memory_space=pltpu.SMEM)
    block = pltpu.VMEM((tokens, 2 * width), BF)
    part = pltpu.VMEM((tokens // ny, 2 * width), BF)
    line = dma((nz, CHUNKS))
    scratch = [
        pltpu.VMEM((nx, nh, ny, nc, depth, 2 * width), BF),
        pltpu.VMEM((depth, 2 * width), BF),
        pltpu.VMEM((depth, 2 * width), BF),
        pltpu.VMEM((nz, lmax, feat), BF),
        pltpu.VMEM((lmax, 2 * width), BF),
        pltpu.VMEM((2, tokens, 2 * width), BF),
        block, block, block, block,
        part, part, part, part, part, part,
        pltpu.VMEM((lmax, 2 * width), F32),
        pltpu.VMEM((lmax, 2 * width), BF),
        pltpu.VMEM((nz, lmax, feat), BF),
        pltpu.VMEM((nz, lmax, feat), BF),
        pltpu.VMEM((2, lmax, feat), F32),
        dma((2, 2, nh, 4)), dma((2, 2, nh, 4)), dma((2, nh, 2, 4)), dma((2, nh, 2, 4)), dma((2, 2)), dma((2, 2, nc)),
        dma((2, nh, 4)), dma((2, nh, 4)), dma((2,)), dma((2,)),
        pltpu.SemaphoreType.REGULAR,
        line, line, line, line,
        dma((1,)), dma((1,)), dma((ny,)), dma((1,)), dma((2, 2)), dma((2, 2)), dma((1,)), dma((ny,)),
        dma((1,)), dma((1,)), dma((ny,)), dma((1,)), dma((2, 2)), dma((2, 2)), dma((1,)), dma((ny,)),
        line, line, line, line,
    ]
    return pl.pallas_call(
        functools.partial(kernel, (nx, nh, ny, nc, nz)),
        out_shape=(
            pltpu.VMEM(queries.shape, BF),
            pltpu.VMEM(queries.shape, BF),
            pltpu.VMEM(encodings.shape, BF),
        ),
        in_specs=[smem, smem] + [vmem] * 5,
        out_specs=(vmem, vmem, vmem),
        scratch_shapes=scratch,
        compiler_params=pltpu.CompilerParams(
            collective_id=0, has_side_effects=True, vmem_limit_bytes=56 * 2**20
        ),
        name="flow_block",
    )(text_length, image_offset, queries, cotangent, encodings, key_weight, value_weight)


def solution(mesh):
    return jax.shard_map(
        functools.partial(shards, mesh.shape["head"]),
        mesh=mesh,
        in_specs=(
            P("seq", "head"),
            P("seq", None, "head"),
            P("seq", "head"),
            P("seq", "head"),
            P("seq"),
            P("seq"),
            P("seq", "head"),
        ),
        out_specs=(P("seq", "head"), P("seq", "head"), P("seq", None, "head")),
        check_vma=False,
    )
```
